32 devices in a mesh: seq: 8 (over z, y), prompt: 4 (over x, core).
Axes of the slice: x: 2, y: 2, z: 4, core: 2. Of those that a mesh axis runs over, the one named last changes fastest.
Arguments:
- queries: bfloat16 [8192, 1024], P(('prompt', 'seq')), parts along dimension 0, may hold values from -6 to 6
- keys: bfloat16 [8192, 1024], P(('prompt', 'seq')), parts along dimension 0, may hold values from -6 to 6
- values: bfloat16 [8192, 1024], P(('prompt', 'seq')), parts along dimension 0, may hold values from -6 to 6
- cotangent: bfloat16 [8192, 1024], P(('prompt', 'seq')), parts along dimension 0, may hold values from -6 to 6
- restrict_one: bfloat16 [8, 256], replicated, may hold values from -0.375 to 0.375
- restrict_two: bfloat16 [4, 256], replicated, may hold values from -0.375 to 0.375
Outputs:
- attended: bfloat16 [8192, 1024], P(('prompt', 'seq')), parts along dimension 0
- grad_q: bfloat16 [8192, 1024], P(('prompt', 'seq')), parts along dimension 0
- grad_k: bfloat16 [8192, 1024], P(('prompt', 'seq')), parts along dimension 0
- grad_v: bfloat16 [8192, 1024], P(('prompt', 'seq')), parts along dimension 0
The draws below stay inside these ranges and needn't reach their ends.
There are 4 independent parts, one for each index of `prompt`. The reference program is written for one: setup_inputs(seed, part) draws one part's arguments, and reference() takes and returns one part's arrays. A program takes and returns all parts, laid end to end along the dimension named above; an argument that names none is the same for every part. Nothing has to cross between parts.
All inputs are finite; a program needn't handle non-finite values.
Results may differ from the reference program's by a relative error of at most 0.02.
Values may be sent and summed in bfloat16 or wider, within the bound.
No kernel may reach another device: no remote copies, remote signals or barrier semaphores. Data moves between devices by JAX's collectives and lax.ppermute only.
A program may use at most 128 MiB of HBM per device.

```python
import math
import jax
import jax.numpy as jnp
from jax import lax

D = 1024
HEADS = 16
HEAD_DIM = 64
BLOCK = 256
COARSE_ONE = 8
COARSE_TWO = 4
SEQ = 2048
N_SEQ = 8


def draw_queries(key, part):
    key = jax.random.fold_in(key, 11)
    return jnp.clip(1.5 * jax.random.normal(key, (SEQ, D), jnp.float32), -6.0, 6.0).astype(jnp.bfloat16)


def draw_keys(key, part):
    key = jax.random.fold_in(key, 12)
    return jnp.clip(1.5 * jax.random.normal(key, (SEQ, D), jnp.float32), -6.0, 6.0).astype(jnp.bfloat16)


def level_of(key, shape, pieces, smallest, top_value):
    def one(position, blocks):
        draws = jax.random.uniform(jax.random.fold_in(jax.random.fold_in(key, 6), position), (blocks,), jnp.float32, smallest / len(pieces), top_value / len(pieces))
        return jnp.repeat(jnp.exp(draws), shape[position] // blocks).reshape((-1,) + (1,) * (len(shape) - position - 1))

    gain = one(*pieces[0])
    for cut in pieces[1:]:
        gain = gain * one(*cut)
    return gain


def normal_values(stream_key, extent, scale, reach, cuts=(), kind=jnp.bfloat16):
    values = jax.random.normal(stream_key, extent, jnp.float32) * scale
    if len(cuts) > 0:
        values = level_of(stream_key, extent, cuts, -0.22, 0.18) * values
    return jnp.clip(values, min=-reach, max=reach).astype(kind)


def setup_inputs(seed: int = 0, part: int = 0) -> dict:
    key_list = jax.random.split(jax.random.key(seed), 7)
    part_keys = jax.random.split(jax.random.fold_in(key_list[6], part), 7)
    return {
        "queries": draw_queries(jax.random.fold_in(jax.random.fold_in(key_list[6], part), 71), part),
        "keys": draw_keys(jax.random.fold_in(jax.random.fold_in(key_list[6], part), 71), part),
        "values": normal_values(part_keys[2], (SEQ, D), 1.0, 6.0, ((0, 8),)),
        "cotangent": normal_values(part_keys[3], (SEQ, D), 1.0, 6.0, ((0, 8),)),
        "restrict_one": normal_values(key_list[4], (COARSE_ONE, BLOCK), BLOCK ** -0.5, 0.375),
        "restrict_two": normal_values(key_list[5], (COARSE_TWO, BLOCK), BLOCK ** -0.5, 0.375),
    }


level_one_bias = math.log(32.0)
level_two_bias = math.log(64.0)
masked_bias = -1e+30

def attend_block(query_block, cotangent_block, key_rows, key_bias):
    row_count = query_block.shape[0]
    key_count = key_rows.shape[0]
    scaling = 1.0 / math.sqrt(HEAD_DIM)
    query_heads = query_block.astype(jnp.float32).reshape(row_count, HEADS, HEAD_DIM)
    cotangent_heads = cotangent_block.astype(jnp.float32).reshape(row_count, HEADS, HEAD_DIM)
    key_heads = key_rows[:, :D].astype(jnp.float32).reshape(key_count, HEADS, HEAD_DIM)
    value_heads = key_rows[:, D:].astype(jnp.float32).reshape(key_count, HEADS, HEAD_DIM)
    scores = jnp.einsum('qhd,khd->hqk', query_heads, key_heads) * scaling + key_bias[None, None, :]
    highest = lax.optimization_barrier(jnp.max(scores, axis=2))
    log_total = highest + jnp.log(lax.optimization_barrier(jnp.sum(jnp.exp(scores - highest[:, :, None]), axis=2)))
    probs = jnp.exp(scores - log_total[:, :, None])
    weights = lax.optimization_barrier(probs.astype(jnp.bfloat16)).astype(jnp.float32)
    attended = jnp.einsum('hqk,khd->qhd', weights, value_heads).astype(jnp.bfloat16)
    attended_wide = lax.optimization_barrier(attended).astype(jnp.float32)
    delta = jnp.einsum('qhd,qhd->hq', cotangent_heads, attended_wide)
    dots = jnp.einsum('qhd,khd->hqk', cotangent_heads, value_heads)
    score_grad = lax.optimization_barrier((probs * (dots - delta[:, :, None])).astype(jnp.bfloat16)).astype(jnp.float32)
    grad_query = (jnp.einsum('hqk,khd->qhd', score_grad, key_heads) * scaling).reshape(row_count, D)
    grad_key = (jnp.einsum('hqk,qhd->khd', score_grad, query_heads) * scaling).reshape(key_count, D)
    grad_value = jnp.einsum('hqk,qhd->khd', weights, cotangent_heads).reshape(key_count, D)
    return (attended.reshape(row_count, D), grad_query.astype(jnp.bfloat16), jnp.concatenate([grad_key, grad_value], axis=1))

def reference(queries, keys, values, cotangent, restrict_one, restrict_two):
    width = 2 * D
    paired = jnp.concatenate([keys, values], axis=1)
    blocks = paired.reshape(N_SEQ, BLOCK, width).astype(jnp.float32)
    coarse_one = jnp.einsum('fb,nbc->nfc', restrict_one.astype(jnp.float32), blocks).astype(jnp.bfloat16)
    coarse_two = jnp.einsum('fb,nbc->nfc', restrict_two.astype(jnp.float32), blocks).astype(jnp.bfloat16)
    paired_padded = jnp.pad(paired, ((BLOCK, BLOCK), (0, 0)))
    one_padded = jnp.pad(coarse_one.reshape(N_SEQ * COARSE_ONE, width), ((3 * COARSE_ONE, 3 * COARSE_ONE), (0, 0)))
    two_all = coarse_two.reshape(N_SEQ * COARSE_TWO, width)
    near_offset = jnp.repeat(jnp.array([-1, 0, 1], dtype=jnp.int32), BLOCK)
    middle_offset = jnp.repeat(jnp.array([-3, -2, 2, 3], dtype=jnp.int32), COARSE_ONE)
    far_block = jnp.repeat(jnp.arange(N_SEQ, dtype=jnp.int32), COARSE_TWO)

    def step(carry, block_index):
        grad_near, grad_middle, grad_far = carry
        start = (block_index * BLOCK).astype(jnp.int32)
        near_keys = lax.dynamic_slice_in_dim(paired_padded, start, 3 * BLOCK, 0)
        window = lax.dynamic_slice_in_dim(one_padded, (block_index * COARSE_ONE).astype(jnp.int32), 7 * COARSE_ONE, 0)
        middle_keys = jnp.concatenate([window[:2 * COARSE_ONE], window[5 * COARSE_ONE:]], axis=0)
        key_rows = jnp.concatenate([near_keys, middle_keys, two_all], axis=0)
        near_place = block_index + near_offset
        middle_place = block_index + middle_offset
        near_valid = (near_place >= 0) & (near_place < N_SEQ)
        middle_valid = (middle_place >= 0) & (middle_place < N_SEQ)
        far_valid = jnp.abs(far_block - block_index) >= 4
        key_bias = jnp.concatenate([jnp.where(near_valid, 0.0, masked_bias), jnp.where(middle_valid, level_one_bias, masked_bias), jnp.where(far_valid, level_two_bias, masked_bias)]).astype(jnp.float32)
        query_block = lax.dynamic_slice_in_dim(queries, start, BLOCK, 0)
        cotangent_block = lax.dynamic_slice_in_dim(cotangent, start, BLOCK, 0)
        attended, grad_query, key_grads = attend_block(query_block, cotangent_block, key_rows, key_bias)
        near_sum = lax.dynamic_slice_in_dim(grad_near, start, 3 * BLOCK, 0) + key_grads[:3 * BLOCK]
        grad_near = lax.dynamic_update_slice_in_dim(grad_near, near_sum, start, 0)
        middle_grads = key_grads[3 * BLOCK:3 * BLOCK + 4 * COARSE_ONE]
        window_grads = jnp.concatenate([middle_grads[:2 * COARSE_ONE], jnp.zeros((3 * COARSE_ONE, width), jnp.float32), middle_grads[2 * COARSE_ONE:]], axis=0)
        middle_start = (block_index * COARSE_ONE).astype(jnp.int32)
        middle_sum = lax.dynamic_slice_in_dim(grad_middle, middle_start, 7 * COARSE_ONE, 0) + window_grads
        grad_middle = lax.dynamic_update_slice_in_dim(grad_middle, middle_sum, middle_start, 0)
        grad_far = grad_far + key_grads[3 * BLOCK + 4 * COARSE_ONE:]
        return ((grad_near, grad_middle, grad_far), (attended, grad_query))
    initial = (jnp.zeros((SEQ + 2 * BLOCK, width), jnp.float32), jnp.zeros(((N_SEQ + 6) * COARSE_ONE, width), jnp.float32), jnp.zeros((N_SEQ * COARSE_TWO, width), jnp.float32))
    (grad_near, grad_middle, grad_far), (attended_blocks, grad_q_blocks) = lax.scan(step, initial, jnp.arange(N_SEQ, dtype=jnp.int32))
    attended = attended_blocks.reshape(SEQ, D)
    grad_q = grad_q_blocks.reshape(SEQ, D)
    fine_grads = grad_near[BLOCK:BLOCK + SEQ].reshape(N_SEQ, BLOCK, width)
    middle_own = grad_middle[3 * COARSE_ONE:3 * COARSE_ONE + N_SEQ * COARSE_ONE].reshape(N_SEQ, COARSE_ONE, width)
    far_own = grad_far.reshape(N_SEQ, COARSE_TWO, width)
    total = fine_grads + jnp.einsum('fb,nfc->nbc', restrict_one.astype(jnp.float32), middle_own, precision=lax.Precision.HIGHEST)
    total = total + jnp.einsum('fb,nfc->nbc', restrict_two.astype(jnp.float32), far_own, precision=lax.Precision.HIGHEST)
    total = total.reshape(SEQ, width)
    return (attended, grad_q, total[:, :D].astype(jnp.bfloat16), total[:, D:].astype(jnp.bfloat16))
```

```python
import math

import jax
import jax.numpy as jnp
from jax import lax
from jax.experimental import pallas as pl
from jax.experimental.pallas import tpu as pltpu
from jax.sharding import PartitionSpec as P

HEAD_DIM = 64
PAIR = 2 * HEAD_DIM
TILE = 32
GRANT = 32 * 1024 * 1024

level_one_bias = math.log(32.0)
level_two_bias = math.log(64.0)
masked_bias = -1e30


def swap_pairs(size):
    return [(i, i ^ 1) for i in range(size)]


def direct_pairs(size):
    return [(i, j) for i in range(size) for j in [i + 2 if i % 2 else i - 2] if 0 <= j < size]


def inverse(pairs):
    return [(j, i) for i, j in pairs]


def shift_pairs(size, shift):
    return [(i, (i + 2 * shift) % size) for i in range(size)]


def dot(a, b):
    return jnp.dot(a, b, preferred_element_type=jnp.float32)


def block_diagonal(both):
    top, bottom = (both[:HEAD_DIM], both[HEAD_DIM:])
    zero = jnp.zeros_like(top)
    return jnp.concatenate(
        [jnp.concatenate([top, zero], axis=1), jnp.concatenate([zero, bottom], axis=1)], axis=0
    )


def stacked_heads(both):
    lane = lax.broadcasted_iota(jnp.int32, both.shape, 1)
    first = lane < HEAD_DIM
    zero = jnp.zeros_like(both)
    return jnp.concatenate([jnp.where(first, both, zero), jnp.where(first, zero, both)], axis=0)


def head_rows(both, h):
    return both[h * HEAD_DIM : (h + 1) * HEAD_DIM]


class Unit:
    def __init__(self, query, cotangent, keys, values, keys_t, values_t, bias):
        scaled = query.astype(jnp.float32) * (1.0 / math.sqrt(HEAD_DIM))
        self.rows = query.shape[0]
        self.keys, self.values, self.keys_t, self.values_t = (keys, values, keys_t, values_t)
        self.bias = bias
        self.query_wide = block_diagonal(scaled.T.astype(jnp.bfloat16))
        self.query_tall = stacked_heads(scaled).astype(jnp.bfloat16)
        self.cotangent_t = cotangent.astype(jnp.float32).T
        self.scores = {}
        self.highest = None
        self.total = 0.0
        self.weights = {}
        self.raw = [0.0, 0.0]
        self.grad_q_t = [0.0, 0.0]
        self.grads = []

    def columns(self, h):
        return slice(h * self.rows, (h + 1) * self.rows)

    def score(self, part):
        score = dot(self.keys[part], self.query_wide)
        plain = max(0, self.keys.shape[0] - self.bias.shape[0] - part.start)
        if plain < score.shape[0]:
            skip = part.start + plain - (self.keys.shape[0] - self.bias.shape[0])
            biased = score[plain:] + self.bias[skip : skip + score.shape[0] - plain]
            score = jnp.concatenate([score[:plain], biased], axis=0) if plain else biased
        highest = jnp.max(score, axis=0, keepdims=True)
        self.highest = highest if self.highest is None else jnp.maximum(self.highest, highest)
        self.scores[part.start] = score

    def weigh(self, part):
        score = self.scores[part.start]
        parts = []
        for start in range(0, score.shape[0], TILE):
            prob = jnp.exp(score[start : start + TILE] - self.highest)
            self.total = self.total + jnp.sum(prob.reshape(-1, 8, prob.shape[1]), axis=0)
            parts.append(prob.astype(jnp.bfloat16))
        weight = jnp.concatenate(parts, axis=0)
        for h in range(2):
            self.raw[h] = self.raw[h] + dot(
                head_rows(self.values_t, h)[:, part], weight[:, self.columns(h)]
            )
        self.weights[part.start] = weight

    def finish(self):
        share = 1.0 / jnp.sum(self.total, axis=0, keepdims=True)
        shares = [share[:, self.columns(h)] for h in range(2)]
        out_t = jnp.concatenate([self.raw[h] * shares[h] for h in range(2)], axis=0)
        self.out = out_t.T.astype(jnp.bfloat16)
        product = self.cotangent_t * out_t.astype(jnp.bfloat16).astype(jnp.float32)
        self.delta = jnp.concatenate(
            [
                jnp.sum(head_rows(product, h), axis=0, keepdims=True) * shares[h]
                for h in range(2)
            ],
            axis=1,
        )
        shared_t = jnp.concatenate(
            [head_rows(self.cotangent_t, h) * shares[h] for h in range(2)], axis=0
        )
        self.cotangent_wide = block_diagonal(shared_t.astype(jnp.bfloat16))
        self.cotangent_tall = stacked_heads(shared_t.T).astype(jnp.bfloat16)

    def differentiate(self, part):
        weight = self.weights[part.start]
        dots = dot(self.values[part], self.cotangent_wide)
        parts = []
        for start in range(0, dots.shape[0], TILE):
            rows = slice(start, start + TILE)
            grad = weight[rows].astype(jnp.float32) * (dots[rows] - self.delta)
            parts.append(grad.astype(jnp.bfloat16))
        score_grad = jnp.concatenate(parts, axis=0)
        self.grads.append((dot(score_grad, self.query_tall), dot(weight, self.cotangent_tall)))
        for h in range(2):
            self.grad_q_t[h] = self.grad_q_t[h] + dot(
                head_rows(self.keys_t, h)[:, part], score_grad[:, self.columns(h)]
            )

    def grad_q(self):
        grad_q_t = jnp.concatenate(self.grad_q_t, axis=0) * (1.0 / math.sqrt(HEAD_DIM))
        return grad_q_t.T.astype(jnp.bfloat16)

    def key_grad(self, n):
        return jnp.concatenate([grads[n] for grads in self.grads], axis=0)


def attention_kernel(shifts):
    def kernel(
        place, bias, q, k, v, c, pair_k, pair_v, relayed_k, relayed_v, pair_qc, direct, *rest
    ):
        coarse = rest[:shifts]
        out, grad_q, pair_out, home_grad, pair_grad, direct_grad, relayed_grad = rest[
            shifts : shifts + 7
        ]
        coarse_grads = rest[shifts + 7 :]
        rows = q.shape[0]

        def halo(have):
            return jnp.full((rows, 1), jnp.where(have > 0, 0.0, masked_bias), jnp.float32)

        def key_rows(n, home, partner, halo):
            far = jnp.concatenate([ref[n] for ref in coarse], axis=0)
            pieces = [home[...], partner[...], halo, far]
            transposed = [piece.T for piece in pieces]
            return jnp.concatenate(pieces, axis=0), jnp.concatenate(transposed, axis=1)

        def unit(query, cotangent, outer_k, outer_v, have, bias):
            keys, keys_t = key_rows(0, k, pair_k, outer_k)
            values, values_t = key_rows(1, v, pair_v, outer_v)
            bias = jnp.concatenate([halo(have), bias], axis=0)
            return Unit(query, cotangent, keys, values, keys_t, values_t, bias)

        one = unit(q[...], c[...], relayed_k[...], relayed_v[...], place[1], bias[0])
        two = unit(pair_qc[0], pair_qc[1], direct[0], direct[1], place[2], bias[1])
        count = one.keys.shape[0]
        middle = count // 32 * 16
        parts = [slice(0, middle), slice(middle, count)]
        for part in parts:
            one.score(part)
        for part in parts:
            two.score(part)
            one.weigh(part)
        one.finish()
        for part in parts:
            one.differentiate(part)
            two.weigh(part)
        two.finish()
        for part in parts:
            two.differentiate(part)
        out[...], grad_q[...] = (one.out, one.grad_q())
        pair_out[0], pair_out[1] = (two.out, two.grad_q())
        for n in range(2):
            first, second = (one.key_grad(n), two.key_grad(n))
            home_grad[n] = first[:rows] + second[:rows]
            pair_grad[n] = first[rows : 2 * rows] + second[rows : 2 * rows]
            relayed_grad[n] = first[2 * rows : 3 * rows].astype(relayed_grad.dtype)
            direct_grad[n] = second[2 * rows : 3 * rows].astype(direct_grad.dtype)
            far_grad = (first[3 * rows :] + second[3 * rows :]).astype(direct_grad.dtype)
            size = far_grad.shape[0] // shifts
            for m, ref in enumerate(coarse_grads):
                ref[n] = far_grad[m * size : (m + 1) * size]

    return kernel


def attention(
    place, bias, q, k, v, c, pair_k, pair_v, relayed_k, relayed_v, pair_qc, direct, coarse
):
    rows, width = q.shape
    columns = width // 2
    steps = columns // PAIR
    shifts = len(coarse)
    coarse_rows = coarse[0].shape[1]

    def mine(j, place):
        return place[0] * steps + j

    def flat(index):
        return pl.BlockSpec((rows, PAIR), index)

    def both(shape_rows):
        return pl.BlockSpec((2, shape_rows, PAIR), lambda j, place: (0, 0, j))

    key_count = 3 * rows + shifts * coarse_rows
    products = 6 * 2 * 2 * rows * key_count * HEAD_DIM * 2 * steps
    bf16, f32 = (jnp.bfloat16, jnp.float32)
    return pl.pallas_call(
        attention_kernel(shifts),
        grid_spec=pltpu.PrefetchScalarGridSpec(
            num_scalar_prefetch=1,
            grid=(steps,),
            in_specs=[pl.BlockSpec(bias.shape, lambda j, place: (0, 0, 0))]
            + [flat(lambda j, place: (0, mine(j, place)))] * 4
            + [flat(lambda j, place: (0, j))] * 4
            + [both(rows)] * 2
            + [both(coarse_rows)] * shifts,
            out_specs=[flat(lambda j, place: (0, j))] * 2
            + [both(rows)] * 5
            + [both(coarse_rows)] * shifts,
        ),
        out_shape=[jax.ShapeDtypeStruct((rows, columns), bf16)] * 2
        + [
            jax.ShapeDtypeStruct((2, rows, columns), bf16),
            jax.ShapeDtypeStruct((2, rows, columns), f32),
            jax.ShapeDtypeStruct((2, rows, columns), f32),
            jax.ShapeDtypeStruct((2, rows, columns), bf16),
            jax.ShapeDtypeStruct((2, rows, columns), bf16),
        ]
        + [jax.ShapeDtypeStruct((2, coarse_rows, columns), bf16)] * shifts,
        compiler_params=pltpu.CompilerParams(vmem_limit_bytes=GRANT),
        cost_estimate=pl.CostEstimate(
            flops=4 * products, bytes_accessed=40 * rows * columns, transcendentals=0
        ),
        name="attention",
    )(
        place, bias, q, k, v, c, pair_k, pair_v, relayed_k, relayed_v, pair_qc, direct, *coarse
    )


def lengthened(restrict, coarse):
    return jnp.einsum(
        "fb,nfc->nbc", restrict.astype(jnp.float32), coarse, precision=lax.Precision.HIGHEST
    )


def per_device(queries, keys, values, cotangent, restrict_one, restrict_two):
    rows, width = queries.shape
    size = lax.axis_size("seq")
    pair_count = size // 2
    position = lax.axis_index("seq")
    parity = lax.rem(position, 2)
    pair = lax.div(position, 2)
    one_rows, two_rows = (restrict_one.shape[0], restrict_two.shape[0])
    block_rows = -(-(one_rows + two_rows) // 16) * 16
    restrict = jnp.concatenate(
        [
            restrict_one,
            restrict_two,
            jnp.zeros((block_rows - one_rows - two_rows, rows), restrict_one.dtype),
        ],
        axis=0,
    )

    shift = jnp.arange(1, pair_count)[:, None, None]
    side = jnp.arange(2)[None, :, None]
    row = jnp.arange(block_rows)[None, None, :]
    sender = lax.rem(pair - shift + pair_count, pair_count)
    block = 2 * sender + jnp.where(side == 0, parity, 1 - parity)

    def coarse_bias(query_block):
        apart = jnp.abs(block - query_block)
        one = (row < one_rows) & (apart >= 2) & (apart <= 3)
        two = (row >= one_rows) & (row < one_rows + two_rows) & (apart >= 4)
        return jnp.where(one, level_one_bias, jnp.where(two, level_two_bias, masked_bias)).reshape(
            -1, 1
        )

    bias = jnp.stack([coarse_bias(position), coarse_bias(2 * pair + 1 - parity)])
    bias = bias.astype(jnp.float32)
    has_before, has_after = (pair > 0, pair < pair_count - 1)
    place = jnp.stack(
        [
            parity,
            jnp.where(parity == 0, has_before, has_after).astype(jnp.int32),
            jnp.where(parity == 0, has_after, has_before).astype(jnp.int32),
        ]
    ).astype(jnp.int32)

    direct_to = direct_pairs(size)
    relayed_to = inverse(direct_to)
    swap = swap_pairs(size)

    def send(value, pairs):
        return lax.ppermute(value, "seq", pairs)

    half = width // 2
    shifts = range(1, pair_count)

    def columns(side, *arrays):
        return [lax.dynamic_slice_in_dim(a, side * half, half, axis=a.ndim - 1) for a in arrays]

    def after(value, *others):
        return lax.optimization_barrier((value, *others))[0]

    pair_k, pair_v = (send(a, swap) for a in columns(1 - parity, keys, values))
    relayed_k = send(pair_k, relayed_to)
    home_kv = jnp.stack(columns(parity, keys, values))
    direct = send(after(home_kv, pair_k), direct_to)
    relayed_v = send(after(pair_v, relayed_k), relayed_to)
    sent_qc = jnp.stack(columns(1 - parity, queries, cotangent))
    pair_qc = send(after(sent_qc, pair_v), swap)
    own_coarse = jnp.concatenate(
        [
            jnp.einsum("fb,nbc->nfc", restrict, home_kv, preferred_element_type=jnp.float32),
            jnp.stack([dot(restrict, pair_k), dot(restrict, pair_v)]),
        ],
        axis=1,
    ).astype(jnp.bfloat16)
    coarse = [send(own_coarse, shift_pairs(size, s)) for s in shifts]
    direct = after(direct, relayed_k)
    relayed_v = after(relayed_v, direct)
    pair_qc = after(pair_qc, relayed_v)
    coarse = after(coarse, pair_qc)

    (
        out, grad_q, pair_out, home_grad, pair_grad, direct_grad, relayed_grad, *coarse_grads,
    ) = attention(
        place, bias, queries, keys, values, cotangent,
        pair_k, pair_v, relayed_k, relayed_v, pair_qc, direct, coarse,
    )

    def whole(own, other):
        axis = own.ndim - 1
        return jnp.where(
            parity == 0,
            jnp.concatenate([own, other], axis=axis),
            jnp.concatenate([other, own], axis=axis),
        )

    relayed_back = send(relayed_grad, direct_to)
    out_back = send(pair_out, swap)
    coarse_back = [send(a, shift_pairs(size, -s)) for s, a in zip(shifts, coarse_grads)]
    pair_total = pair_grad + relayed_back.astype(jnp.float32)
    far = sum(piece.astype(jnp.float32) for piece in after(coarse_back, pair_total))
    pair_total = pair_total + lengthened(restrict, far[:, block_rows:])
    pair_total = pair_total.astype(jnp.bfloat16)
    grad_back = send(pair_total, swap)
    direct_back = send(after(direct_grad, pair_total), relayed_to)
    home_total = home_grad + direct_back.astype(jnp.float32)
    home_total = home_total + lengthened(restrict, far[:, :block_rows])
    home_total = home_total.astype(jnp.bfloat16)
    return (
        whole(out, out_back[0]),
        whole(grad_q, out_back[1]),
        whole(home_total[0], grad_back[0]),
        whole(home_total[1], grad_back[1]),
    )


def solution(mesh):
    split = P(("prompt", "seq"), None)
    return jax.shard_map(
        per_device,
        mesh=mesh,
        in_specs=(split, split, split, split, P(), P()),
        out_specs=(split, split, split, split),
        check_vma=False,
    )
```

```python
import math

import jax
import jax.numpy as jnp
from jax import lax
from jax.experimental import pallas as pl
from jax.experimental.pallas import tpu as pltpu
from jax.sharding import PartitionSpec as P

HEAD_DIM = 64
PAIR = 2 * HEAD_DIM
TILE = 32
GRANT = 32 * 1024 * 1024

level_one_bias = math.log(32.0)
level_two_bias = math.log(64.0)
masked_bias = -1e30


def swap_pairs(size):
    return [(i, i ^ 1) for i in range(size)]


def direct_pairs(size):
    return [(i, j) for i in range(size) for j in [i + 2 if i % 2 else i - 2] if 0 <= j < size]


def inverse(pairs):
    return [(j, i) for i, j in pairs]


def shift_pairs(size, shift):
    return [(i, (i + 2 * shift) % size) for i in range(size)]


def doublings(pair_count):
    steps = []
    held = 1
    while held < pair_count:
        steps.append((held, min(held, pair_count - held)))
        held += steps[-1][1]
    return steps


def dot(a, b):
    return jnp.dot(a, b, preferred_element_type=jnp.float32)


def block_diagonal(both):
    top, bottom = (both[:HEAD_DIM], both[HEAD_DIM:])
    zero = jnp.zeros_like(top)
    return jnp.concatenate(
        [jnp.concatenate([top, zero], axis=1), jnp.concatenate([zero, bottom], axis=1)], axis=0
    )


def stacked_heads(both):
    lane = lax.broadcasted_iota(jnp.int32, both.shape, 1)
    first = lane < HEAD_DIM
    zero = jnp.zeros_like(both)
    return jnp.concatenate([jnp.where(first, both, zero), jnp.where(first, zero, both)], axis=0)


def head_rows(both, h):
    return both[h * HEAD_DIM : (h + 1) * HEAD_DIM]


class Unit:
    def __init__(self, query, cotangent, keys, values, keys_t, values_t, bias):
        scaled = query.astype(jnp.float32) * (1.0 / math.sqrt(HEAD_DIM))
        self.rows = query.shape[0]
        self.keys, self.values, self.keys_t, self.values_t = (keys, values, keys_t, values_t)
        self.bias = bias
        self.query_wide = block_diagonal(scaled.T.astype(jnp.bfloat16))
        self.query_tall = stacked_heads(scaled).astype(jnp.bfloat16)
        self.cotangent_t = cotangent.astype(jnp.float32).T
        self.scores = {}
        self.highest = None
        self.total = 0.0
        self.weights = {}
        self.raw = [0.0, 0.0]
        self.grad_q_t = [0.0, 0.0]
        self.grads = []

    def columns(self, h):
        return slice(h * self.rows, (h + 1) * self.rows)

    def score(self, part):
        score = dot(self.keys[part], self.query_wide)
        plain = max(0, self.keys.shape[0] - self.bias.shape[0] - part.start)
        if plain < score.shape[0]:
            skip = part.start + plain - (self.keys.shape[0] - self.bias.shape[0])
            biased = score[plain:] + self.bias[skip : skip + score.shape[0] - plain]
            score = jnp.concatenate([score[:plain], biased], axis=0) if plain else biased
        highest = jnp.max(score, axis=0, keepdims=True)
        self.highest = highest if self.highest is None else jnp.maximum(self.highest, highest)
        self.scores[part.start] = score

    def weigh(self, part):
        score = self.scores[part.start]
        parts = []
        for start in range(0, score.shape[0], TILE):
            prob = jnp.exp(score[start : start + TILE] - self.highest)
            self.total = self.total + jnp.sum(prob.reshape(-1, 8, prob.shape[1]), axis=0)
            parts.append(prob.astype(jnp.bfloat16))
        weight = jnp.concatenate(parts, axis=0)
        for h in range(2):
            self.raw[h] = self.raw[h] + dot(
                head_rows(self.values_t, h)[:, part], weight[:, self.columns(h)]
            )
        self.weights[part.start] = weight

    def finish(self):
        share = 1.0 / jnp.sum(self.total, axis=0, keepdims=True)
        shares = [share[:, self.columns(h)] for h in range(2)]
        out_t = jnp.concatenate([self.raw[h] * shares[h] for h in range(2)], axis=0)
        self.out = out_t.T.astype(jnp.bfloat16)
        product = self.cotangent_t * out_t.astype(jnp.bfloat16).astype(jnp.float32)
        self.delta = jnp.concatenate(
            [
                jnp.sum(head_rows(product, h), axis=0, keepdims=True) * shares[h]
                for h in range(2)
            ],
            axis=1,
        )
        shared_t = jnp.concatenate(
            [head_rows(self.cotangent_t, h) * shares[h] for h in range(2)], axis=0
        )
        self.cotangent_wide = block_diagonal(shared_t.astype(jnp.bfloat16))
        self.cotangent_tall = stacked_heads(shared_t.T).astype(jnp.bfloat16)

    def differentiate(self, part):
        weight = self.weights[part.start]
        dots = dot(self.values[part], self.cotangent_wide)
        parts = []
        for start in range(0, dots.shape[0], TILE):
            rows = slice(start, start + TILE)
            grad = weight[rows].astype(jnp.float32) * (dots[rows] - self.delta)
            parts.append(grad.astype(jnp.bfloat16))
        score_grad = jnp.concatenate(parts, axis=0)
        self.grads.append((dot(score_grad, self.query_tall), dot(weight, self.cotangent_tall)))
        for h in range(2):
            self.grad_q_t[h] = self.grad_q_t[h] + dot(
                head_rows(self.keys_t, h)[:, part], score_grad[:, self.columns(h)]
            )

    def grad_q(self):
        grad_q_t = jnp.concatenate(self.grad_q_t, axis=0) * (1.0 / math.sqrt(HEAD_DIM))
        return grad_q_t.T.astype(jnp.bfloat16)

    def key_grad(self, n):
        return jnp.concatenate([grads[n] for grads in self.grads], axis=0)


def attention_kernel(shifts):
    def kernel(
        place, bias, q, k, v, c, pair_k, pair_v, relayed_k, relayed_v, pair_qc, direct, *rest
    ):
        coarse = rest[:shifts]
        out, grad_q, pair_out, home_grad, pair_grad, direct_grad, relayed_grad = rest[
            shifts : shifts + 7
        ]
        coarse_grads = rest[shifts + 7 :]
        rows = q.shape[0]

        def halo(have):
            return jnp.full((rows, 1), jnp.where(have > 0, 0.0, masked_bias), jnp.float32)

        def key_rows(n, home, partner, halo):
            far = jnp.concatenate([ref[n] for ref in coarse], axis=0)
            pieces = [home[...], partner[...], halo, far]
            transposed = [piece.T for piece in pieces]
            return jnp.concatenate(pieces, axis=0), jnp.concatenate(transposed, axis=1)

        def unit(query, cotangent, outer_k, outer_v, have, bias):
            keys, keys_t = key_rows(0, k, pair_k, outer_k)
            values, values_t = key_rows(1, v, pair_v, outer_v)
            bias = jnp.concatenate([halo(have), bias], axis=0)
            return Unit(query, cotangent, keys, values, keys_t, values_t, bias)

        one = unit(q[...], c[...], relayed_k[...], relayed_v[...], place[1], bias[0])
        two = unit(pair_qc[0], pair_qc[1], direct[0], direct[1], place[2], bias[1])
        count = one.keys.shape[0]
        middle = count // 32 * 16
        parts = [slice(0, middle), slice(middle, count)]
        for part in parts:
            one.score(part)
        for part in parts:
            two.score(part)
            one.weigh(part)
        one.finish()
        for part in parts:
            one.differentiate(part)
            two.weigh(part)
        two.finish()
        for part in parts:
            two.differentiate(part)
        out[...], grad_q[...] = (one.out, one.grad_q())
        pair_out[0], pair_out[1] = (two.out, two.grad_q())
        for n in range(2):
            first, second = (one.key_grad(n), two.key_grad(n))
            home_grad[n] = first[:rows] + second[:rows]
            pair_grad[n] = first[rows : 2 * rows] + second[rows : 2 * rows]
            relayed_grad[n] = first[2 * rows : 3 * rows].astype(relayed_grad.dtype)
            direct_grad[n] = second[2 * rows : 3 * rows].astype(direct_grad.dtype)
            far_grad = (first[3 * rows :] + second[3 * rows :]).astype(direct_grad.dtype)
            size = far_grad.shape[0] // shifts
            far_grads = [far_grad[m * size : (m + 1) * size] for m in range(shifts)]
            for ref, (distance, count) in zip(coarse_grads, doublings(shifts + 1)):
                for m in range(count):
                    ref[m, n] = far_grads[distance - 1 + m]

    return kernel


def attention(
    place, bias, q, k, v, c, pair_k, pair_v, relayed_k, relayed_v, pair_qc, direct, coarse
):
    rows, width = q.shape
    columns = width // 2
    steps = columns // PAIR
    shifts = len(coarse)
    coarse_rows = coarse[0].shape[1]

    def mine(j, place):
        return place[0] * steps + j

    def flat(index):
        return pl.BlockSpec((rows, PAIR), index)

    def both(shape_rows):
        return pl.BlockSpec((2, shape_rows, PAIR), lambda j, place: (0, 0, j))

    key_count = 3 * rows + shifts * coarse_rows
    products = 6 * 2 * 2 * rows * key_count * HEAD_DIM * 2 * steps
    bf16, f32 = (jnp.bfloat16, jnp.float32)
    return pl.pallas_call(
        attention_kernel(shifts),
        grid_spec=pltpu.PrefetchScalarGridSpec(
            num_scalar_prefetch=1,
            grid=(steps,),
            in_specs=[pl.BlockSpec(bias.shape, lambda j, place: (0, 0, 0))]
            + [flat(lambda j, place: (0, mine(j, place)))] * 4
            + [flat(lambda j, place: (0, j))] * 4
            + [both(rows)] * 2
            + [both(coarse_rows)] * shifts,
            out_specs=[flat(lambda j, place: (0, j))] * 2
            + [both(rows)] * 5
            + [
                pl.BlockSpec((count, 2, coarse_rows, PAIR), lambda j, place: (0, 0, 0, j))
                for _, count in doublings(shifts + 1)
            ],
        ),
        out_shape=[jax.ShapeDtypeStruct((rows, columns), bf16)] * 2
        + [
            jax.ShapeDtypeStruct((2, rows, columns), bf16),
            jax.ShapeDtypeStruct((2, rows, columns), f32),
            jax.ShapeDtypeStruct((2, rows, columns), f32),
            jax.ShapeDtypeStruct((2, rows, columns), bf16),
            jax.ShapeDtypeStruct((2, rows, columns), bf16),
        ]
        + [
            jax.ShapeDtypeStruct((count, 2, coarse_rows, columns), bf16)
            for _, count in doublings(shifts + 1)
        ],
        compiler_params=pltpu.CompilerParams(vmem_limit_bytes=GRANT),
        cost_estimate=pl.CostEstimate(
            flops=4 * products, bytes_accessed=40 * rows * columns, transcendentals=0
        ),
        name="attention",
    )(
        place, bias, q, k, v, c, pair_k, pair_v, relayed_k, relayed_v, pair_qc, direct, *coarse
    )


def lengthened(restrict, coarse):
    return jnp.einsum(
        "fb,nfc->nbc", restrict.astype(jnp.float32), coarse, precision=lax.Precision.HIGHEST
    )


def per_device(queries, keys, values, cotangent, restrict_one, restrict_two):
    rows, width = queries.shape
    size = lax.axis_size("seq")
    pair_count = size // 2
    position = lax.axis_index("seq")
    parity = lax.rem(position, 2)
    pair = lax.div(position, 2)
    one_rows, two_rows = (restrict_one.shape[0], restrict_two.shape[0])
    block_rows = -(-(one_rows + two_rows) // 16) * 16
    restrict = jnp.concatenate(
        [
            restrict_one,
            restrict_two,
            jnp.zeros((block_rows - one_rows - two_rows, rows), restrict_one.dtype),
        ],
        axis=0,
    )

    shift = jnp.arange(1, pair_count)[:, None, None]
    side = jnp.arange(2)[None, :, None]
    row = jnp.arange(block_rows)[None, None, :]
    sender = lax.rem(pair - shift + pair_count, pair_count)
    block = 2 * sender + jnp.where(side == 0, parity, 1 - parity)

    def coarse_bias(query_block):
        apart = jnp.abs(block - query_block)
        one = (row < one_rows) & (apart >= 2) & (apart <= 3)
        two = (row >= one_rows) & (row < one_rows + two_rows) & (apart >= 4)
        return jnp.where(one, level_one_bias, jnp.where(two, level_two_bias, masked_bias)).reshape(
            -1, 1
        )

    bias = jnp.stack([coarse_bias(position), coarse_bias(2 * pair + 1 - parity)])
    bias = bias.astype(jnp.float32)
    has_before, has_after = (pair > 0, pair < pair_count - 1)
    place = jnp.stack(
        [
            parity,
            jnp.where(parity == 0, has_before, has_after).astype(jnp.int32),
            jnp.where(parity == 0, has_after, has_before).astype(jnp.int32),
        ]
    ).astype(jnp.int32)

    direct_to = direct_pairs(size)
    relayed_to = inverse(direct_to)
    swap = swap_pairs(size)

    def send(value, pairs):
        return lax.ppermute(value, "seq", pairs)

    half = width // 2
    shifts = range(1, pair_count)

    def columns(side, *arrays):
        return [lax.dynamic_slice_in_dim(a, side * half, half, axis=a.ndim - 1) for a in arrays]

    def after(value, *others):
        return lax.optimization_barrier((value, *others))[0]

    pair_k, pair_v = (send(a, swap) for a in columns(1 - parity, keys, values))
    relayed_k = send(pair_k, relayed_to)
    home_kv = jnp.stack(columns(parity, keys, values))
    direct = send(after(home_kv, pair_v), direct_to)
    relayed_v = send(after(pair_v, relayed_k), relayed_to)
    sent_qc = jnp.stack(columns(1 - parity, queries, cotangent))
    pair_qc = send(after(sent_qc, pair_v), swap)
    own_coarse = jnp.concatenate(
        [
            jnp.einsum("fb,nbc->nfc", restrict, home_kv, preferred_element_type=jnp.float32),
            jnp.stack([dot(restrict, pair_k), dot(restrict, pair_v)]),
        ],
        axis=1,
    ).astype(jnp.bfloat16)
    coarse = [send(own_coarse, shift_pairs(size, s)) for s in shifts]
    pair_qc = after(pair_qc, relayed_v)
    direct = after(direct, pair_qc)
    coarse = after(coarse, direct)

    (
        out, grad_q, pair_out, home_grad, pair_grad, direct_grad, relayed_grad, *coarse_grads,
    ) = attention(
        place, bias, queries, keys, values, cotangent,
        pair_k, pair_v, relayed_k, relayed_v, pair_qc, direct, coarse,
    )

    def whole(own, other):
        axis = own.ndim - 1
        return jnp.where(
            parity == 0,
            jnp.concatenate([own, other], axis=axis),
            jnp.concatenate([other, own], axis=axis),
        )

    relayed_back = send(relayed_grad, direct_to)
    out_back = send(pair_out, swap)
    direct_back = send(direct_grad, relayed_to)
    pair_total = (pair_grad + relayed_back.astype(jnp.float32)).astype(jnp.bfloat16)
    grad_back = send(pair_total, swap)

    far = None
    for (distance, count), piece in reversed(list(zip(doublings(pair_count), coarse_grads))):
        if far is not None:
            piece = piece.astype(jnp.float32) + far[distance : distance + count]
        piece = piece.astype(jnp.bfloat16)
        back = send(piece, shift_pairs(size, -distance))
        back = back if far is not None else after(back, pair_total)
        back = jnp.pad(back.astype(jnp.float32), [(0, distance - count)] + [(0, 0)] * 3)
        far = back if far is None else far[:distance] + back
    far = far[0]
    other_far = send(far[:, block_rows:].astype(jnp.bfloat16), swap).astype(jnp.float32)
    out_back = after(out_back, piece)
    own_longer = lengthened(restrict, far[:, :block_rows])
    other_longer = lax.optimization_barrier(lengthened(restrict, other_far))
    home_total = home_grad + direct_back.astype(jnp.float32) + own_longer
    home_total = home_total.astype(jnp.bfloat16)

    def summed(n):
        other = grad_back[n].astype(jnp.float32) + other_longer[n]
        return whole(home_total[n], other.astype(jnp.bfloat16))

    return whole(out, out_back[0]), whole(grad_q, out_back[1]), summed(0), summed(1)


def solution(mesh):
    split = P(("prompt", "seq"), None)
    return jax.shard_map(
        per_device,
        mesh=mesh,
        in_specs=(split, split, split, split, P(), P()),
        out_specs=(split, split, split, split),
        check_vma=False,
    )
```

```python
import math

import jax
import jax.numpy as jnp
from jax import lax
from jax.experimental import pallas as pl
from jax.experimental.pallas import tpu as pltpu
from jax.sharding import PartitionSpec as P

HEAD_DIM = 64
PAIR = 2 * HEAD_DIM
TILE = 32
GRANT = 32 * 1024 * 1024

level_one_bias = math.log(32.0)
level_two_bias = math.log(64.0)
masked_bias = -1e30


def swap_pairs(size):
    return [(i, i ^ 1) for i in range(size)]


def direct_pairs(size):
    return [(i, j) for i in range(size) for j in [i + 2 if i % 2 else i - 2] if 0 <= j < size]


def inverse(pairs):
    return [(j, i) for i, j in pairs]


def shift_pairs(size, shift):
    return [(i, (i + 2 * shift) % size) for i in range(size)]


def doublings(pair_count):
    steps = []
    held = 1
    while held < pair_count:
        steps.append((held, min(held, pair_count - held)))
        held += steps[-1][1]
    return steps


def dot(a, b):
    return jnp.dot(a, b, preferred_element_type=jnp.float32)


def block_diagonal(both):
    top, bottom = (both[:HEAD_DIM], both[HEAD_DIM:])
    zero = jnp.zeros_like(top)
    return jnp.concatenate(
        [jnp.concatenate([top, zero], axis=1), jnp.concatenate([zero, bottom], axis=1)], axis=0
    )


def stacked_heads(both):
    lane = lax.broadcasted_iota(jnp.int32, both.shape, 1)
    first = lane < HEAD_DIM
    zero = jnp.zeros_like(both)
    return jnp.concatenate([jnp.where(first, both, zero), jnp.where(first, zero, both)], axis=0)


def head_rows(both, h):
    return both[h * HEAD_DIM : (h + 1) * HEAD_DIM]


class Unit:
    def __init__(self, query, cotangent, keys, values, keys_t, values_t, bias):
        scaled = query.astype(jnp.float32) * (1.0 / math.sqrt(HEAD_DIM))
        scaled = scaled.astype(jnp.bfloat16)
        self.rows = query.shape[0]
        self.keys, self.values, self.keys_t, self.values_t = (keys, values, keys_t, values_t)
        self.bias = bias
        self.query_wide = block_diagonal(scaled.T)
        self.query_tall = stacked_heads(scaled)
        self.cotangent_t = cotangent.T.astype(jnp.float32)
        self.scores = {}
        self.highest = None
        self.total = 0.0
        self.weights = {}
        self.raw = [0.0, 0.0]
        self.grad_q_t = [0.0, 0.0]
        self.grads = []

    def columns(self, h):
        return slice(h * self.rows, (h + 1) * self.rows)

    def score(self, part):
        score = dot(self.keys[part], self.query_wide)
        plain = max(0, self.keys.shape[0] - self.bias.shape[0] - part.start)
        if plain < score.shape[0]:
            skip = part.start + plain - (self.keys.shape[0] - self.bias.shape[0])
            biased = score[plain:] + self.bias[skip : skip + score.shape[0] - plain]
            score = jnp.concatenate([score[:plain], biased], axis=0) if plain else biased
        highest = jnp.max(score, axis=0, keepdims=True)
        self.highest = highest if self.highest is None else jnp.maximum(self.highest, highest)
        self.scores[part.start] = score

    def weigh(self, part):
        score = self.scores[part.start]
        parts = []
        for start in range(0, score.shape[0], TILE):
            prob = jnp.exp(score[start : start + TILE] - self.highest)
            self.total = self.total + jnp.sum(prob.reshape(-1, 8, prob.shape[1]), axis=0)
            parts.append(prob.astype(jnp.bfloat16))
        weight = jnp.concatenate(parts, axis=0)
        for h in range(2):
            self.raw[h] = self.raw[h] + dot(
                head_rows(self.values_t, h)[:, part], weight[:, self.columns(h)]
            )
        self.weights[part.start] = weight

    def finish(self):
        share = 1.0 / jnp.sum(self.total, axis=0, keepdims=True)
        shares = [share[:, self.columns(h)] for h in range(2)]
        out_t = jnp.concatenate([self.raw[h] * shares[h] for h in range(2)], axis=0)
        out_t = out_t.astype(jnp.bfloat16)
        self.out = out_t.T
        product = self.cotangent_t * out_t.astype(jnp.float32)
        self.delta = jnp.concatenate(
            [
                jnp.sum(head_rows(product, h), axis=0, keepdims=True) * shares[h]
                for h in range(2)
            ],
            axis=1,
        )
        shared_t = jnp.concatenate(
            [head_rows(self.cotangent_t, h) * shares[h] for h in range(2)], axis=0
        )
        shared_t = shared_t.astype(jnp.bfloat16)
        self.cotangent_wide = block_diagonal(shared_t)
        self.cotangent_tall = stacked_heads(shared_t.T)

    def differentiate(self, part):
        weight = self.weights[part.start]
        dots = dot(self.values[part], self.cotangent_wide)
        parts = []
        for start in range(0, dots.shape[0], TILE):
            rows = slice(start, start + TILE)
            grad = weight[rows].astype(jnp.float32) * (dots[rows] - self.delta)
            parts.append(grad.astype(jnp.bfloat16))
        score_grad = jnp.concatenate(parts, axis=0)
        self.grads.append((dot(score_grad, self.query_tall), dot(weight, self.cotangent_tall)))
        for h in range(2):
            self.grad_q_t[h] = self.grad_q_t[h] + dot(
                head_rows(self.keys_t, h)[:, part], score_grad[:, self.columns(h)]
            )

    def grad_q(self):
        grad_q_t = jnp.concatenate(self.grad_q_t, axis=0) * (1.0 / math.sqrt(HEAD_DIM))
        return grad_q_t.astype(jnp.bfloat16).T

    def key_grad(self, n):
        return jnp.concatenate([grads[n] for grads in self.grads], axis=0)


def attention_kernel(shifts):
    def kernel(
        place, bias, q, k, v, c, pair_k, pair_v, relayed_k, relayed_v, pair_qc, direct, *rest
    ):
        coarse = rest[:shifts]
        out, grad_q, pair_out, home_grad, pair_grad, direct_grad, relayed_grad = rest[
            shifts : shifts + 7
        ]
        coarse_grads = rest[shifts + 7 :]
        rows = q.shape[0]

        def halo(have):
            return jnp.full((rows, 1), jnp.where(have > 0, 0.0, masked_bias), jnp.float32)

        def chunk(pieces):
            return jnp.concatenate(pieces, axis=0), jnp.concatenate([a.T for a in pieces], axis=1)

        def shared(n, home, partner):
            far = jnp.concatenate([ref[n] for ref in coarse], axis=0)
            return chunk([home[...], partner[...]]), chunk([far])

        both_keys, both_values = (shared(0, k, pair_k), shared(1, v, pair_v))

        def key_rows(outer, near_far):
            near, far = near_far
            pieces = [near, chunk([outer]), far]
            return [jnp.concatenate([a[n] for a in pieces], axis=n) for n in range(2)]

        def unit(query, cotangent, outer_k, outer_v, have, bias):
            keys, keys_t = key_rows(outer_k, both_keys)
            values, values_t = key_rows(outer_v, both_values)
            bias = jnp.concatenate([halo(have), bias], axis=0)
            return Unit(query, cotangent, keys, values, keys_t, values_t, bias)

        one = unit(q[...], c[...], relayed_k[...], relayed_v[...], place[1], bias[0])
        two = unit(pair_qc[0], pair_qc[1], direct[0], direct[1], place[2], bias[1])
        count = one.keys.shape[0]
        middle = count // 32 * 16
        parts = [slice(0, middle), slice(middle, count)]
        for part in parts:
            one.score(part)
        for part in parts:
            two.score(part)
            one.weigh(part)
        one.finish()
        for part in parts:
            one.differentiate(part)
            two.weigh(part)
        two.finish()
        for part in parts:
            two.differentiate(part)
        out[...], grad_q[...] = (one.out, one.grad_q())
        pair_out[0], pair_out[1] = (two.out, two.grad_q())
        for n in range(2):
            first, second = (one.key_grad(n), two.key_grad(n))
            home_grad[n] = first[:rows] + second[:rows]
            pair_grad[n] = first[rows : 2 * rows] + second[rows : 2 * rows]
            relayed_grad[n] = first[2 * rows : 3 * rows].astype(relayed_grad.dtype)
            direct_grad[n] = second[2 * rows : 3 * rows].astype(direct_grad.dtype)
            far_grad = (first[3 * rows :] + second[3 * rows :]).astype(direct_grad.dtype)
            size = far_grad.shape[0] // shifts
            far_grads = [far_grad[m * size : (m + 1) * size] for m in range(shifts)]
            for ref, (distance, count) in zip(coarse_grads, doublings(shifts + 1)):
                for m in range(count):
                    ref[m, n] = far_grads[distance - 1 + m]

    return kernel


def attention(
    place, bias, q, k, v, c, pair_k, pair_v, relayed_k, relayed_v, pair_qc, direct, coarse
):
    rows, width = q.shape
    columns = width // 2
    steps = columns // PAIR
    shifts = len(coarse)
    coarse_rows = coarse[0].shape[1]

    def mine(j, place):
        return place[0] * steps + j

    def flat(index):
        return pl.BlockSpec((rows, PAIR), index)

    def both(shape_rows):
        return pl.BlockSpec((2, shape_rows, PAIR), lambda j, place: (0, 0, j))

    key_count = 3 * rows + shifts * coarse_rows
    products = 6 * 2 * 2 * rows * key_count * HEAD_DIM * 2 * steps
    bf16, f32 = (jnp.bfloat16, jnp.float32)
    return pl.pallas_call(
        attention_kernel(shifts),
        grid_spec=pltpu.PrefetchScalarGridSpec(
            num_scalar_prefetch=1,
            grid=(steps,),
            in_specs=[pl.BlockSpec(bias.shape, lambda j, place: (0, 0, 0))]
            + [flat(lambda j, place: (0, mine(j, place)))] * 4
            + [flat(lambda j, place: (0, j))] * 4
            + [both(rows)] * 2
            + [both(coarse_rows)] * shifts,
            out_specs=[flat(lambda j, place: (0, j))] * 2
            + [both(rows)] * 5
            + [
                pl.BlockSpec((count, 2, coarse_rows, PAIR), lambda j, place: (0, 0, 0, j))
                for _, count in doublings(shifts + 1)
            ],
        ),
        out_shape=[jax.ShapeDtypeStruct((rows, columns), bf16)] * 2
        + [
            jax.ShapeDtypeStruct((2, rows, columns), bf16),
            jax.ShapeDtypeStruct((2, rows, columns), f32),
            jax.ShapeDtypeStruct((2, rows, columns), f32),
            jax.ShapeDtypeStruct((2, rows, columns), bf16),
            jax.ShapeDtypeStruct((2, rows, columns), bf16),
        ]
        + [
            jax.ShapeDtypeStruct((count, 2, coarse_rows, columns), bf16)
            for _, count in doublings(shifts + 1)
        ],
        compiler_params=pltpu.CompilerParams(vmem_limit_bytes=GRANT),
        cost_estimate=pl.CostEstimate(
            flops=4 * products, bytes_accessed=40 * rows * columns, transcendentals=0
        ),
        name="attention",
    )(
        place, bias, q, k, v, c, pair_k, pair_v, relayed_k, relayed_v, pair_qc, direct, *coarse
    )


def lengthened(restrict, coarse):
    return jnp.einsum(
        "fb,nfc->nbc", restrict.astype(jnp.float32), coarse, precision=lax.Precision.HIGHEST
    )


def per_device(queries, keys, values, cotangent, restrict_one, restrict_two):
    rows, width = queries.shape
    size = lax.axis_size("seq")
    pair_count = size // 2
    position = lax.axis_index("seq")
    parity = lax.rem(position, 2)
    pair = lax.div(position, 2)
    one_rows, two_rows = (restrict_one.shape[0], restrict_two.shape[0])
    block_rows = -(-(one_rows + two_rows) // 16) * 16
    restrict = jnp.concatenate(
        [
            restrict_one,
            restrict_two,
            jnp.zeros((block_rows - one_rows - two_rows, rows), restrict_one.dtype),
        ],
        axis=0,
    )

    shift = jnp.arange(1, pair_count)[:, None, None]
    side = jnp.arange(2)[None, :, None]
    row = jnp.arange(block_rows)[None, None, :]
    sender = lax.rem(pair - shift + pair_count, pair_count)
    block = 2 * sender + jnp.where(side == 0, parity, 1 - parity)

    def coarse_bias(query_block):
        apart = jnp.abs(block - query_block)
        one = (row < one_rows) & (apart >= 2) & (apart <= 3)
        two = (row >= one_rows) & (row < one_rows + two_rows) & (apart >= 4)
        return jnp.where(one, level_one_bias, jnp.where(two, level_two_bias, masked_bias)).reshape(
            -1, 1
        )

    bias = jnp.stack([coarse_bias(position), coarse_bias(2 * pair + 1 - parity)])
    bias = bias.astype(jnp.float32)
    has_before, has_after = (pair > 0, pair < pair_count - 1)
    place = jnp.stack(
        [
            parity,
            jnp.where(parity == 0, has_before, has_after).astype(jnp.int32),
            jnp.where(parity == 0, has_after, has_before).astype(jnp.int32),
        ]
    ).astype(jnp.int32)

    direct_to = direct_pairs(size)
    relayed_to = inverse(direct_to)
    swap = swap_pairs(size)

    def send(value, pairs):
        return lax.ppermute(value, "seq", pairs)

    half = width // 2
    shifts = range(1, pair_count)

    def columns(side, *arrays):
        return [lax.dynamic_slice_in_dim(a, side * half, half, axis=a.ndim - 1) for a in arrays]

    def after(value, *others):
        return lax.optimization_barrier((value, *others))[0]

    pair_k, pair_v = (send(a, swap) for a in columns(1 - parity, keys, values))
    relayed_k = send(pair_k, relayed_to)
    home_kv = jnp.stack(columns(parity, keys, values))
    direct = send(after(home_kv, pair_k), direct_to)
    relayed_v = send(after(pair_v, relayed_k), relayed_to)
    sent_qc = jnp.stack(columns(1 - parity, queries, cotangent))
    pair_qc = send(after(sent_qc, pair_v), swap)
    own_coarse = jnp.concatenate(
        [
            jnp.einsum("fb,nbc->nfc", restrict, home_kv, preferred_element_type=jnp.float32),
            jnp.stack([dot(restrict, pair_k), dot(restrict, pair_v)]),
        ],
        axis=1,
    ).astype(jnp.bfloat16)
    coarse = [send(own_coarse, shift_pairs(size, s)) for s in shifts]
    direct = after(direct, relayed_k)
    relayed_v = after(relayed_v, direct)
    pair_qc = after(pair_qc, relayed_v)
    coarse = after(coarse, pair_qc)

    (
        out, grad_q, pair_out, home_grad, pair_grad, direct_grad, relayed_grad, *coarse_grads,
    ) = attention(
        place, bias, queries, keys, values, cotangent,
        pair_k, pair_v, relayed_k, relayed_v, pair_qc, direct, coarse,
    )

    def whole(own, other):
        axis = own.ndim - 1
        return jnp.where(
            parity == 0,
            jnp.concatenate([own, other], axis=axis),
            jnp.concatenate([other, own], axis=axis),
        )

    relayed_back = send(relayed_grad, direct_to)
    out_back = send(pair_out, swap)
    direct_back = send(direct_grad, relayed_to)
    pair_total = (pair_grad + relayed_back.astype(jnp.float32)).astype(jnp.bfloat16)
    grad_back = send(pair_total, swap)

    far = None
    for (distance, count), piece in reversed(list(zip(doublings(pair_count), coarse_grads))):
        if far is not None:
            piece = piece.astype(jnp.float32) + far[distance : distance + count]
        piece = piece.astype(jnp.bfloat16)
        back = send(piece, shift_pairs(size, -distance))
        back = back if far is not None else after(back, pair_total)
        back = jnp.pad(back.astype(jnp.float32), [(0, distance - count)] + [(0, 0)] * 3)
        far = back if far is None else far[:distance] + back
    far = far[0]
    other_far = send(far[:, block_rows:].astype(jnp.bfloat16), swap).astype(jnp.float32)
    out_back = after(out_back, piece)
    own_longer = lengthened(restrict, far[:, :block_rows])
    other_longer = lax.optimization_barrier(lengthened(restrict, other_far))
    home_total = home_grad + direct_back.astype(jnp.float32) + own_longer
    home_total = home_total.astype(jnp.bfloat16)

    def summed(n):
        other = grad_back[n].astype(jnp.float32) + other_longer[n]
        return whole(home_total[n], other.astype(jnp.bfloat16))

    return whole(out, out_back[0]), whole(grad_q, out_back[1]), summed(0), summed(1)


def solution(mesh):
    split = P(("prompt", "seq"), None)
    return jax.shard_map(
        per_device,
        mesh=mesh,
        in_specs=(split, split, split, split, P(), P()),
        out_specs=(split, split, split, split),
        check_vma=False,
    )
```

```python
import math

import jax
import jax.numpy as jnp
from jax import lax
from jax.experimental import pallas as pl
from jax.experimental.pallas import tpu as pltpu
from jax.sharding import PartitionSpec as P

HEAD_DIM = 64
PAIR = 2 * HEAD_DIM
TILE = 32
GRANT = 32 * 1024 * 1024

level_one_bias = math.log(32.0)
level_two_bias = math.log(64.0)
masked_bias = -1e30


def swap_pairs(size):
    return [(i, i ^ 1) for i in range(size)]


def direct_pairs(size):
    return [(i, j) for i in range(size) for j in [i + 2 if i % 2 else i - 2] if 0 <= j < size]


def inverse(pairs):
    return [(j, i) for i, j in pairs]


def shift_pairs(size, shift):
    return [(i, (i + 2 * shift) % size) for i in range(size)]


def doublings(pair_count):
    steps = []
    held = 1
    while held < pair_count:
        steps.append((held, min(held, pair_count - held)))
        held += steps[-1][1]
    return steps


def dot(a, b):
    return jnp.dot(a, b, preferred_element_type=jnp.float32)


def block_diagonal(both):
    top, bottom = (both[:HEAD_DIM], both[HEAD_DIM:])
    zero = jnp.zeros_like(top)
    return jnp.concatenate(
        [jnp.concatenate([top, zero], axis=1), jnp.concatenate([zero, bottom], axis=1)], axis=0
    )


def stacked_heads(both):
    lane = lax.broadcasted_iota(jnp.int32, both.shape, 1)
    first = lane < HEAD_DIM
    zero = jnp.zeros_like(both)
    return jnp.concatenate([jnp.where(first, both, zero), jnp.where(first, zero, both)], axis=0)


def head_rows(both, h):
    return both[h * HEAD_DIM : (h + 1) * HEAD_DIM]


class Unit:
    def __init__(self, query, cotangent, keys, values, keys_t, values_t, bias):
        scaled = query.astype(jnp.float32) * (1.0 / math.sqrt(HEAD_DIM))
        scaled = scaled.astype(jnp.bfloat16)
        self.rows = query.shape[0]
        self.keys, self.values, self.keys_t, self.values_t = (keys, values, keys_t, values_t)
        self.bias = bias
        self.query_wide = block_diagonal(scaled.T)
        self.query_tall = stacked_heads(scaled)
        self.cotangent_t = cotangent.T.astype(jnp.float32)
        self.scores = {}
        self.highest = None
        self.total = 0.0
        self.weights = {}
        self.raw = [0.0, 0.0]
        self.grad_q_t = [0.0, 0.0]
        self.grads = []

    def columns(self, h):
        return slice(h * self.rows, (h + 1) * self.rows)

    def score(self, part):
        score = dot(self.keys[part], self.query_wide)
        plain = max(0, self.keys.shape[0] - self.bias.shape[0] - part.start)
        if plain < score.shape[0]:
            skip = part.start + plain - (self.keys.shape[0] - self.bias.shape[0])
            biased = score[plain:] + self.bias[skip : skip + score.shape[0] - plain]
            score = jnp.concatenate([score[:plain], biased], axis=0) if plain else biased
        highest = jnp.max(score, axis=0, keepdims=True)
        self.highest = highest if self.highest is None else jnp.maximum(self.highest, highest)
        self.scores[part.start] = score

    def weigh(self, part):
        score = self.scores[part.start]
        parts = []
        for start in range(0, score.shape[0], TILE):
            prob = jnp.exp(score[start : start + TILE] - self.highest)
            self.total = self.total + jnp.sum(prob.reshape(-1, 8, prob.shape[1]), axis=0)
            parts.append(prob.astype(jnp.bfloat16))
        weight = jnp.concatenate(parts, axis=0)
        for h in range(2):
            self.raw[h] = self.raw[h] + dot(
                head_rows(self.values_t, h)[:, part], weight[:, self.columns(h)]
            )
        self.weights[part.start] = weight

    def finish(self):
        share = 1.0 / jnp.sum(self.total, axis=0, keepdims=True)
        shares = [share[:, self.columns(h)] for h in range(2)]
        out_t = jnp.concatenate([self.raw[h] * shares[h] for h in range(2)], axis=0)
        out_t = out_t.astype(jnp.bfloat16)
        self.out = out_t.T
        product = self.cotangent_t * out_t.astype(jnp.float32)
        self.delta = jnp.concatenate(
            [
                jnp.sum(head_rows(product, h), axis=0, keepdims=True) * shares[h]
                for h in range(2)
            ],
            axis=1,
        )
        shared_t = jnp.concatenate(
            [head_rows(self.cotangent_t, h) * shares[h] for h in range(2)], axis=0
        )
        shared_t = shared_t.astype(jnp.bfloat16)
        self.cotangent_wide = block_diagonal(shared_t)
        self.cotangent_tall = stacked_heads(shared_t.T)

    def differentiate(self, part):
        weight = self.weights[part.start]
        dots = dot(self.values[part], self.cotangent_wide)
        parts = []
        for start in range(0, dots.shape[0], TILE):
            rows = slice(start, start + TILE)
            grad = weight[rows].astype(jnp.float32) * (dots[rows] - self.delta)
            parts.append(grad.astype(jnp.bfloat16))
        score_grad = jnp.concatenate(parts, axis=0)
        self.grads.append((dot(score_grad, self.query_tall), dot(weight, self.cotangent_tall)))
        for h in range(2):
            self.grad_q_t[h] = self.grad_q_t[h] + dot(
                head_rows(self.keys_t, h)[:, part], score_grad[:, self.columns(h)]
            )

    def grad_q(self):
        grad_q_t = jnp.concatenate(self.grad_q_t, axis=0) * (1.0 / math.sqrt(HEAD_DIM))
        return grad_q_t.astype(jnp.bfloat16).T

    def key_grad(self, n):
        return jnp.concatenate([grads[n] for grads in self.grads], axis=0)


def attention_kernel(shifts, one_rows, two_rows):
    def kernel(
        place, q, k, v, c, pair_k, pair_v, relayed_k, relayed_v, pair_qc, direct, pair_coarse, *rest
    ):
        coarse = rest[:shifts]
        out, grad_q, pair_out, home_grad, pair_grad, direct_grad, relayed_grad = rest[
            shifts : shifts + 7
        ]
        coarse_grads = rest[shifts + 7 :]
        rows = q.shape[0]

        parity, pair = (place[0], place[3])
        coarse_rows = pair_coarse.shape[2]

        def halo(have):
            return jnp.full((rows, 2 * rows), jnp.where(have > 0, 0.0, masked_bias), jnp.float32)

        def coarse_bias(query_block):
            row = lax.broadcasted_iota(jnp.int32, (coarse_rows, 2 * rows), 0)
            pieces = []
            for side in (parity, 1 - parity):
                for shift in range(1, shifts + 1):
                    sender = jnp.where(pair >= shift, pair - shift, pair - shift + shifts + 1)
                    apart = jnp.abs(2 * sender + side - query_block)
                    one = jnp.where((apart == 2) | (apart == 3), level_one_bias, masked_bias)
                    two = jnp.where(apart >= 4, level_two_bias, masked_bias)
                    rest = jnp.where(row < one_rows + two_rows, two, masked_bias)
                    pieces.append(jnp.where(row < one_rows, one, rest))
            return jnp.concatenate(pieces, axis=0).astype(jnp.float32)

        def chunk(pieces):
            return jnp.concatenate(pieces, axis=0), jnp.concatenate([a.T for a in pieces], axis=1)

        def shared(n, home, partner):
            far = [ref[0, n] for ref in coarse] + [pair_coarse[m, n] for m in range(shifts)]
            far = jnp.concatenate(far, axis=0)
            return chunk([home[...], partner[...]]), chunk([far])

        both_keys, both_values = (shared(0, k, pair_k), shared(1, v, pair_v))

        def key_rows(outer, near_far):
            near, far = near_far
            pieces = [near, chunk([outer]), far]
            return [jnp.concatenate([a[n] for a in pieces], axis=n) for n in range(2)]

        def unit(query, cotangent, outer_k, outer_v, have, bias):
            keys, keys_t = key_rows(outer_k, both_keys)
            values, values_t = key_rows(outer_v, both_values)
            bias = jnp.concatenate([halo(have), bias], axis=0)
            return Unit(query, cotangent, keys, values, keys_t, values_t, bias)

        one = unit(q[...], c[...], relayed_k[...], relayed_v[...], place[1], coarse_bias(2 * pair + parity))
        two = unit(pair_qc[0], pair_qc[1], direct[0], direct[1], place[2], coarse_bias(2 * pair + 1 - parity))
        count = one.keys.shape[0]
        middle = count // 32 * 16
        parts = [slice(0, middle), slice(middle, count)]
        for part in parts:
            one.score(part)
        for part in parts:
            two.score(part)
            one.weigh(part)
        one.finish()
        for part in parts:
            one.differentiate(part)
            two.weigh(part)
        two.finish()
        for part in parts:
            two.differentiate(part)
        out[...], grad_q[...] = (one.out, one.grad_q())
        pair_out[0], pair_out[1] = (two.out, two.grad_q())
        for n in range(2):
            first, second = (one.key_grad(n), two.key_grad(n))
            home_grad[n] = first[:rows] + second[:rows]
            pair_grad[n] = first[rows : 2 * rows] + second[rows : 2 * rows]
            relayed_grad[n] = first[2 * rows : 3 * rows].astype(relayed_grad.dtype)
            direct_grad[n] = second[2 * rows : 3 * rows].astype(direct_grad.dtype)
            far_grad = (first[3 * rows :] + second[3 * rows :]).astype(direct_grad.dtype)
            for ref, (distance, count) in zip(coarse_grads, doublings(shifts + 1)):
                for m in range(count):
                    for side in range(2):
                        start = (side * shifts + distance - 1 + m) * coarse_rows
                        piece = far_grad[start : start + coarse_rows]
                        ref[m, n, side * coarse_rows : (side + 1) * coarse_rows] = piece

    return kernel


def attention(
    place, level_rows, q, k, v, c, pair_k, pair_v, relayed_k, relayed_v, pair_qc, direct, pair_coarse, coarse
):
    rows, width = q.shape
    columns = width // 2
    steps = columns // PAIR
    shifts = len(coarse)
    coarse_rows = pair_coarse.shape[2]

    def mine(j, place):
        return place[0] * steps + j

    def flat(index):
        return pl.BlockSpec((rows, PAIR), index)

    def both(shape_rows):
        return pl.BlockSpec((2, shape_rows, PAIR), lambda j, place: (0, 0, j))

    key_count = 3 * rows + 2 * shifts * coarse_rows
    products = 6 * 2 * 2 * rows * key_count * HEAD_DIM * 2 * steps
    bf16, f32 = (jnp.bfloat16, jnp.float32)
    return pl.pallas_call(
        attention_kernel(shifts, *level_rows),
        grid_spec=pltpu.PrefetchScalarGridSpec(
            num_scalar_prefetch=1,
            grid=(steps,),
            in_specs=[flat(lambda j, place: (0, mine(j, place)))] * 4
            + [flat(lambda j, place: (0, j))] * 4
            + [both(rows)] * 2
            + [pl.BlockSpec((shifts, 2, coarse_rows, PAIR), lambda j, place: (0, 0, 0, j))]
            + [pl.BlockSpec((1, 2, coarse_rows, PAIR), lambda j, place: (place[0], 0, 0, j))]
            * shifts,
            out_specs=[flat(lambda j, place: (0, j))] * 2
            + [both(rows)] * 5
            + [
                pl.BlockSpec((count, 2, 2 * coarse_rows, PAIR), lambda j, place: (0, 0, 0, j))
                for _, count in doublings(shifts + 1)
            ],
        ),
        out_shape=[jax.ShapeDtypeStruct((rows, columns), bf16)] * 2
        + [
            jax.ShapeDtypeStruct((2, rows, columns), bf16),
            jax.ShapeDtypeStruct((2, rows, columns), f32),
            jax.ShapeDtypeStruct((2, rows, columns), f32),
            jax.ShapeDtypeStruct((2, rows, columns), bf16),
            jax.ShapeDtypeStruct((2, rows, columns), bf16),
        ]
        + [
            jax.ShapeDtypeStruct((count, 2, 2 * coarse_rows, columns), bf16)
            for _, count in doublings(shifts + 1)
        ],
        compiler_params=pltpu.CompilerParams(vmem_limit_bytes=GRANT),
        cost_estimate=pl.CostEstimate(
            flops=4 * products, bytes_accessed=40 * rows * columns, transcendentals=0
        ),
        name="attention",
    )(
        place, q, k, v, c, pair_k, pair_v, relayed_k, relayed_v, pair_qc, direct, pair_coarse, *coarse
    )


def restrict_kernel(restrict, k, v, out):
    half = out.shape[3]
    for n, ref in enumerate((k, v)):
        for side in range(2):
            columns = ref[:, side * half : (side + 1) * half]
            out[side, n] = dot(restrict[...], columns).astype(out.dtype)


def restricted(restrict, keys, values):
    vmem = pl.BlockSpec(memory_space=pltpu.VMEM)
    return pl.pallas_call(
        restrict_kernel,
        in_specs=[vmem] * 3,
        out_specs=vmem,
        out_shape=jax.ShapeDtypeStruct(
            (2, 2, restrict.shape[0], keys.shape[1] // 2), keys.dtype
        ),
        compiler_params=pltpu.CompilerParams(vmem_limit_bytes=GRANT),
        name="restrict",
    )(restrict, keys, values)


def lengthened(restrict, coarse):
    return jnp.einsum(
        "fb,nfc->nbc", restrict.astype(jnp.float32), coarse, precision=lax.Precision.HIGHEST
    )


def per_device(queries, keys, values, cotangent, restrict_one, restrict_two):
    rows, width = queries.shape
    size = lax.axis_size("seq")
    pair_count = size // 2
    position = lax.axis_index("seq")
    parity = lax.rem(position, 2)
    pair = lax.div(position, 2)
    one_rows, two_rows = (restrict_one.shape[0], restrict_two.shape[0])
    block_rows = -(-(one_rows + two_rows) // 16) * 16
    restrict = jnp.concatenate(
        [
            restrict_one,
            restrict_two,
            jnp.zeros((block_rows - one_rows - two_rows, rows), restrict_one.dtype),
        ],
        axis=0,
    )

    has_before, has_after = (pair > 0, pair < pair_count - 1)
    place = jnp.stack(
        [
            parity,
            jnp.where(parity == 0, has_before, has_after).astype(jnp.int32),
            jnp.where(parity == 0, has_after, has_before).astype(jnp.int32),
            pair,
        ]
    ).astype(jnp.int32)

    direct_to = direct_pairs(size)
    relayed_to = inverse(direct_to)
    swap = swap_pairs(size)

    def send(value, pairs):
        return lax.ppermute(value, "seq", pairs)

    half = width // 2
    shifts = range(1, pair_count)

    def columns(side, *arrays):
        return [lax.dynamic_slice_in_dim(a, side * half, half, axis=a.ndim - 1) for a in arrays]

    def after(value, *others):
        return lax.optimization_barrier((value, *others))[0]

    pair_k, pair_v = (send(a, swap) for a in columns(1 - parity, keys, values))
    own_coarse = after(restricted(restrict, keys, values), pair_k)
    coarse = [send(own_coarse, shift_pairs(size, s)) for s in shifts]
    relayed_k = send(pair_k, relayed_to)
    home_kv = jnp.stack(columns(parity, keys, values))
    direct = send(after(home_kv, pair_k), direct_to)
    sent_qc = jnp.stack(columns(1 - parity, queries, cotangent))
    pair_qc = send(after(sent_qc, pair_v), swap)
    relayed_v = send(after(pair_v, relayed_k), relayed_to)
    sent_coarse = jnp.concatenate(
        [lax.dynamic_slice_in_dim(a, 1 - parity, 1) for a in after(coarse, pair_v)], axis=0
    )
    pair_coarse = send(sent_coarse, swap)
    relayed_v = after(relayed_v, direct)
    pair_qc = after(pair_qc, relayed_v)

    (
        out, grad_q, pair_out, home_grad, pair_grad, direct_grad, relayed_grad, *coarse_grads,
    ) = attention(
        place, (one_rows, two_rows), queries, keys, values, cotangent,
        pair_k, pair_v, relayed_k, relayed_v, pair_qc, direct, pair_coarse, coarse,
    )

    def whole(own, other):
        axis = own.ndim - 1
        return jnp.where(
            parity == 0,
            jnp.concatenate([own, other], axis=axis),
            jnp.concatenate([other, own], axis=axis),
        )

    relayed_back = send(relayed_grad, direct_to)
    out_back = send(pair_out, swap)
    direct_back = send(direct_grad, relayed_to)
    pair_total = (pair_grad + relayed_back.astype(jnp.float32)).astype(jnp.bfloat16)
    grad_back = send(pair_total, swap)

    far = None
    for (distance, count), piece in reversed(list(zip(doublings(pair_count), coarse_grads))):
        if far is not None:
            piece = piece.astype(jnp.float32) + far[distance : distance + count]
        piece = piece.astype(jnp.bfloat16)
        back = send(piece, shift_pairs(size, -distance))
        back = back if far is not None else after(back, pair_total)
        back = jnp.pad(back.astype(jnp.float32), [(0, distance - count)] + [(0, 0)] * 3)
        far = back if far is None else far[:distance] + back
    far = far[0]
    other_far = send(far[:, block_rows:].astype(jnp.bfloat16), swap).astype(jnp.float32)
    out_back = after(out_back, piece)
    own_longer = lengthened(restrict, far[:, :block_rows])
    other_longer = lax.optimization_barrier(lengthened(restrict, other_far))
    home_total = home_grad + direct_back.astype(jnp.float32) + own_longer
    home_total = home_total.astype(jnp.bfloat16)

    def summed(n):
        other = grad_back[n].astype(jnp.float32) + other_longer[n]
        return whole(home_total[n], other.astype(jnp.bfloat16))

    return whole(out, out_back[0]), whole(grad_q, out_back[1]), summed(0), summed(1)


def solution(mesh):
    split = P(("prompt", "seq"), None)
    return jax.shard_map(
        per_device,
        mesh=mesh,
        in_specs=(split, split, split, split, P(), P()),
        out_specs=(split, split, split, split),
        check_vma=False,
    )
```

```python
import math

import jax
import jax.numpy as jnp
from jax import lax
from jax.experimental import pallas as pl
from jax.experimental.pallas import tpu as pltpu
from jax.sharding import PartitionSpec as P

HEAD_DIM = 64
PAIR = 2 * HEAD_DIM
TILE = 32
GRANT = 32 * 1024 * 1024

level_one_bias = math.log(32.0)
level_two_bias = math.log(64.0)
masked_bias = -1e30


def swap_pairs(size):
    return [(i, i ^ 1) for i in range(size)]


def direct_pairs(size):
    return [(i, j) for i in range(size) for j in [i + 2 if i % 2 else i - 2] if 0 <= j < size]


def inverse(pairs):
    return [(j, i) for i, j in pairs]


def shift_pairs(size, shift):
    return [(i, (i + 2 * shift) % size) for i in range(size)]


def doublings(pair_count):
    steps = []
    held = 1
    while held < pair_count:
        steps.append((held, min(held, pair_count - held)))
        held += steps[-1][1]
    return steps


def dot(a, b):
    return jnp.dot(a, b, preferred_element_type=jnp.float32)


def block_diagonal(both):
    top, bottom = (both[:HEAD_DIM], both[HEAD_DIM:])
    zero = jnp.zeros_like(top)
    return jnp.concatenate(
        [jnp.concatenate([top, zero], axis=1), jnp.concatenate([zero, bottom], axis=1)], axis=0
    )


def stacked_heads(both):
    lane = lax.broadcasted_iota(jnp.int32, both.shape, 1)
    first = lane < HEAD_DIM
    zero = jnp.zeros_like(both)
    return jnp.concatenate([jnp.where(first, both, zero), jnp.where(first, zero, both)], axis=0)


def head_rows(both, h):
    return both[h * HEAD_DIM : (h + 1) * HEAD_DIM]


class Unit:
    def __init__(self, query, cotangent, keys, values, keys_t, values_t, bias):
        scaled = query.astype(jnp.float32) * (1.0 / math.sqrt(HEAD_DIM))
        scaled = scaled.astype(jnp.bfloat16)
        self.rows = query.shape[0]
        self.keys, self.values, self.keys_t, self.values_t = (keys, values, keys_t, values_t)
        self.bias = bias
        self.query_wide = block_diagonal(scaled.T)
        self.query_tall = stacked_heads(scaled)
        self.cotangent_t = cotangent.T.astype(jnp.float32)
        self.scores = {}
        self.highest = None
        self.total = 0.0
        self.weights = {}
        self.raw = [0.0, 0.0]
        self.grad_q_t = [0.0, 0.0]
        self.grads = []

    def columns(self, h):
        return slice(h * self.rows, (h + 1) * self.rows)

    def score(self, part):
        score = dot(self.keys[part], self.query_wide)
        plain = max(0, self.keys.shape[0] - self.bias.shape[0] - part.start)
        if plain < score.shape[0]:
            skip = part.start + plain - (self.keys.shape[0] - self.bias.shape[0])
            biased = score[plain:] + self.bias[skip : skip + score.shape[0] - plain]
            score = jnp.concatenate([score[:plain], biased], axis=0) if plain else biased
        highest = jnp.max(score, axis=0, keepdims=True)
        self.highest = highest if self.highest is None else jnp.maximum(self.highest, highest)
        self.scores[part.start] = score

    def weigh(self, part):
        score = self.scores[part.start]
        parts = []
        for start in range(0, score.shape[0], TILE):
            prob = jnp.exp(score[start : start + TILE] - self.highest)
            self.total = self.total + jnp.sum(prob.reshape(-1, 8, prob.shape[1]), axis=0)
            parts.append(prob.astype(jnp.bfloat16))
        weight = jnp.concatenate(parts, axis=0)
        for h in range(2):
            self.raw[h] = self.raw[h] + dot(
                head_rows(self.values_t, h)[:, part], weight[:, self.columns(h)]
            )
        self.weights[part.start] = weight

    def finish(self):
        share = 1.0 / jnp.sum(self.total, axis=0, keepdims=True)
        shares = [share[:, self.columns(h)] for h in range(2)]
        out_t = jnp.concatenate([self.raw[h] * shares[h] for h in range(2)], axis=0)
        out_t = out_t.astype(jnp.bfloat16)
        self.out = out_t.T
        product = self.cotangent_t * out_t.astype(jnp.float32)
        self.delta = jnp.concatenate(
            [
                jnp.sum(head_rows(product, h), axis=0, keepdims=True) * shares[h]
                for h in range(2)
            ],
            axis=1,
        )
        shared_t = jnp.concatenate(
            [head_rows(self.cotangent_t, h) * shares[h] for h in range(2)], axis=0
        )
        shared_t = shared_t.astype(jnp.bfloat16)
        self.cotangent_wide = block_diagonal(shared_t)
        self.cotangent_tall = stacked_heads(shared_t.T)

    def differentiate(self, part):
        weight = self.weights[part.start]
        dots = dot(self.values[part], self.cotangent_wide)
        parts = []
        for start in range(0, dots.shape[0], TILE):
            rows = slice(start, start + TILE)
            grad = weight[rows].astype(jnp.float32) * (dots[rows] - self.delta)
            parts.append(grad.astype(jnp.bfloat16))
        score_grad = jnp.concatenate(parts, axis=0)
        self.grads.append((dot(score_grad, self.query_tall), dot(weight, self.cotangent_tall)))
        for h in range(2):
            self.grad_q_t[h] = self.grad_q_t[h] + dot(
                head_rows(self.keys_t, h)[:, part], score_grad[:, self.columns(h)]
            )

    def grad_q(self):
        grad_q_t = jnp.concatenate(self.grad_q_t, axis=0) * (1.0 / math.sqrt(HEAD_DIM))
        return grad_q_t.astype(jnp.bfloat16).T

    def key_grad(self, n):
        return jnp.concatenate([grads[n] for grads in self.grads], axis=0)


def attention_kernel(shifts, one_rows, two_rows):
    def kernel(
        place, q, k, v, c, pair_k, pair_v, relayed_k, relayed_v, pair_qc, direct, pair_coarse, *rest
    ):
        coarse = rest[:shifts]
        out, grad_q, pair_out, home_grad, pair_grad, direct_grad, relayed_grad = rest[
            shifts : shifts + 7
        ]
        coarse_grads = rest[shifts + 7 :]
        rows = q.shape[0]

        parity, pair = (place[0], place[3])
        coarse_rows = pair_coarse.shape[2]

        def halo(have):
            return jnp.full((rows, 2 * rows), jnp.where(have > 0, 0.0, masked_bias), jnp.float32)

        def coarse_bias(query_block):
            row = lax.broadcasted_iota(jnp.int32, (coarse_rows, 2 * rows), 0)
            pieces = []
            for side in (parity, 1 - parity):
                for shift in range(1, shifts + 1):
                    sender = jnp.where(pair >= shift, pair - shift, pair - shift + shifts + 1)
                    apart = jnp.abs(2 * sender + side - query_block)
                    one = jnp.where((apart == 2) | (apart == 3), level_one_bias, masked_bias)
                    two = jnp.where(apart >= 4, level_two_bias, masked_bias)
                    rest = jnp.where(row < one_rows + two_rows, two, masked_bias)
                    pieces.append(jnp.where(row < one_rows, one, rest))
            return jnp.concatenate(pieces, axis=0).astype(jnp.float32)

        def chunk(pieces):
            return jnp.concatenate(pieces, axis=0), jnp.concatenate([a.T for a in pieces], axis=1)

        def shared(n, home, partner):
            far = [ref[0, n] for ref in coarse] + [pair_coarse[m, n] for m in range(shifts)]
            far = jnp.concatenate(far, axis=0)
            return chunk([home[...], partner[...]]), chunk([far])

        both_keys, both_values = (shared(0, k, pair_k), shared(1, v, pair_v))

        def key_rows(outer, near_far):
            near, far = near_far
            pieces = [near, chunk([outer]), far]
            return [jnp.concatenate([a[n] for a in pieces], axis=n) for n in range(2)]

        def unit(query, cotangent, outer_k, outer_v, have, bias):
            keys, keys_t = key_rows(outer_k, both_keys)
            values, values_t = key_rows(outer_v, both_values)
            bias = jnp.concatenate([halo(have), bias], axis=0)
            return Unit(query, cotangent, keys, values, keys_t, values_t, bias)

        one = unit(q[...], c[...], relayed_k[...], relayed_v[...], place[1], coarse_bias(2 * pair + parity))
        two = unit(pair_qc[0], pair_qc[1], direct[0], direct[1], place[2], coarse_bias(2 * pair + 1 - parity))
        count = one.keys.shape[0]
        parts = [slice(0, count)]
        for part in parts:
            one.score(part)
        for part in parts:
            two.score(part)
            one.weigh(part)
        one.finish()
        for part in parts:
            one.differentiate(part)
            two.weigh(part)
        two.finish()
        for part in parts:
            two.differentiate(part)
        out[...], grad_q[...] = (one.out, one.grad_q())
        pair_out[0], pair_out[1] = (two.out, two.grad_q())
        for n in range(2):
            first, second = (one.key_grad(n), two.key_grad(n))
            home_grad[n] = first[:rows] + second[:rows]
            pair_grad[n] = first[rows : 2 * rows] + second[rows : 2 * rows]
            relayed_grad[n] = first[2 * rows : 3 * rows].astype(relayed_grad.dtype)
            direct_grad[n] = second[2 * rows : 3 * rows].astype(direct_grad.dtype)
            far_grad = (first[3 * rows :] + second[3 * rows :]).astype(direct_grad.dtype)
            for ref, (distance, count) in zip(coarse_grads, doublings(shifts + 1)):
                for m in range(count):
                    for side in range(2):
                        start = (side * shifts + distance - 1 + m) * coarse_rows
                        piece = far_grad[start : start + coarse_rows]
                        ref[m, n, side * coarse_rows : (side + 1) * coarse_rows] = piece

    return kernel


def attention(
    place, level_rows, q, k, v, c, pair_k, pair_v, relayed_k, relayed_v, pair_qc, direct, pair_coarse, coarse
):
    rows, width = q.shape
    columns = width // 2
    steps = columns // PAIR
    shifts = len(coarse)
    coarse_rows = pair_coarse.shape[2]

    def mine(j, place):
        return place[0] * steps + j

    def flat(index):
        return pl.BlockSpec((rows, PAIR), index)

    def both(shape_rows):
        return pl.BlockSpec((2, shape_rows, PAIR), lambda j, place: (0, 0, j))

    key_count = 3 * rows + 2 * shifts * coarse_rows
    products = 6 * 2 * 2 * rows * key_count * HEAD_DIM * 2 * steps
    bf16, f32 = (jnp.bfloat16, jnp.float32)
    return pl.pallas_call(
        attention_kernel(shifts, *level_rows),
        grid_spec=pltpu.PrefetchScalarGridSpec(
            num_scalar_prefetch=1,
            grid=(steps,),
            in_specs=[flat(lambda j, place: (0, mine(j, place)))] * 4
            + [flat(lambda j, place: (0, j))] * 4
            + [both(rows)] * 2
            + [pl.BlockSpec((shifts, 2, coarse_rows, PAIR), lambda j, place: (0, 0, 0, j))]
            + [pl.BlockSpec((1, 2, coarse_rows, PAIR), lambda j, place: (place[0], 0, 0, j))]
            * shifts,
            out_specs=[flat(lambda j, place: (0, j))] * 2
            + [both(rows)] * 5
            + [
                pl.BlockSpec((count, 2, 2 * coarse_rows, PAIR), lambda j, place: (0, 0, 0, j))
                for _, count in doublings(shifts + 1)
            ],
        ),
        out_shape=[jax.ShapeDtypeStruct((rows, columns), bf16)] * 2
        + [
            jax.ShapeDtypeStruct((2, rows, columns), bf16),
            jax.ShapeDtypeStruct((2, rows, columns), f32),
            jax.ShapeDtypeStruct((2, rows, columns), f32),
            jax.ShapeDtypeStruct((2, rows, columns), bf16),
            jax.ShapeDtypeStruct((2, rows, columns), bf16),
        ]
        + [
            jax.ShapeDtypeStruct((count, 2, 2 * coarse_rows, columns), bf16)
            for _, count in doublings(shifts + 1)
        ],
        compiler_params=pltpu.CompilerParams(vmem_limit_bytes=GRANT),
        cost_estimate=pl.CostEstimate(
            flops=4 * products, bytes_accessed=40 * rows * columns, transcendentals=0
        ),
        name="attention",
    )(
        place, q, k, v, c, pair_k, pair_v, relayed_k, relayed_v, pair_qc, direct, pair_coarse, *coarse
    )


def restrict_kernel(restrict, k, v, out):
    half = out.shape[3]
    for n, ref in enumerate((k, v)):
        for side in range(2):
            columns = ref[:, side * half : (side + 1) * half]
            out[side, n] = dot(restrict[...], columns).astype(out.dtype)


def restricted(restrict, keys, values):
    vmem = pl.BlockSpec(memory_space=pltpu.VMEM)
    return pl.pallas_call(
        restrict_kernel,
        in_specs=[vmem] * 3,
        out_specs=vmem,
        out_shape=jax.ShapeDtypeStruct(
            (2, 2, restrict.shape[0], keys.shape[1] // 2), keys.dtype
        ),
        compiler_params=pltpu.CompilerParams(vmem_limit_bytes=GRANT),
        name="restrict",
    )(restrict, keys, values)


def lengthened(restrict, coarse):
    return jnp.einsum(
        "fb,nfc->nbc", restrict.astype(jnp.float32), coarse, precision=lax.Precision.HIGHEST
    )


def per_device(queries, keys, values, cotangent, restrict_one, restrict_two):
    rows, width = queries.shape
    size = lax.axis_size("seq")
    pair_count = size // 2
    position = lax.axis_index("seq")
    parity = lax.rem(position, 2)
    pair = lax.div(position, 2)
    one_rows, two_rows = (restrict_one.shape[0], restrict_two.shape[0])
    block_rows = -(-(one_rows + two_rows) // 16) * 16
    restrict = jnp.concatenate(
        [
            restrict_one,
            restrict_two,
            jnp.zeros((block_rows - one_rows - two_rows, rows), restrict_one.dtype),
        ],
        axis=0,
    )

    has_before, has_after = (pair > 0, pair < pair_count - 1)
    place = jnp.stack(
        [
            parity,
            jnp.where(parity == 0, has_before, has_after).astype(jnp.int32),
            jnp.where(parity == 0, has_after, has_before).astype(jnp.int32),
            pair,
        ]
    ).astype(jnp.int32)

    direct_to = direct_pairs(size)
    relayed_to = inverse(direct_to)
    swap = swap_pairs(size)

    def send(value, pairs):
        return lax.ppermute(value, "seq", pairs)

    half = width // 2
    shifts = range(1, pair_count)

    def columns(side, *arrays):
        return [lax.dynamic_slice_in_dim(a, side * half, half, axis=a.ndim - 1) for a in arrays]

    def after(value, *others):
        return lax.optimization_barrier((value, *others))[0]

    pair_k, pair_v = (send(a, swap) for a in columns(1 - parity, keys, values))
    own_coarse = after(restricted(restrict, keys, values), pair_k)
    coarse = [send(own_coarse, shift_pairs(size, s)) for s in shifts]
    relayed_k = send(pair_k, relayed_to)
    home_kv = jnp.stack(columns(parity, keys, values))
    direct = send(after(home_kv, pair_k), direct_to)
    sent_qc = jnp.stack(columns(1 - parity, queries, cotangent))
    pair_qc = send(after(sent_qc, pair_v), swap)
    relayed_v = send(after(pair_v, relayed_k), relayed_to)
    sent_coarse = jnp.concatenate(
        [lax.dynamic_slice_in_dim(a, 1 - parity, 1) for a in after(coarse, pair_v)], axis=0
    )
    pair_coarse = send(sent_coarse, swap)
    relayed_v = after(relayed_v, direct)
    pair_qc = after(pair_qc, relayed_v)

    (
        out, grad_q, pair_out, home_grad, pair_grad, direct_grad, relayed_grad, *coarse_grads,
    ) = attention(
        place, (one_rows, two_rows), queries, keys, values, cotangent,
        pair_k, pair_v, relayed_k, relayed_v, pair_qc, direct, pair_coarse, coarse,
    )

    def whole(own, other):
        axis = own.ndim - 1
        return jnp.where(
            parity == 0,
            jnp.concatenate([own, other], axis=axis),
            jnp.concatenate([other, own], axis=axis),
        )

    relayed_back = send(relayed_grad, direct_to)
    out_back = send(pair_out, swap)
    direct_back = send(direct_grad, relayed_to)

    far = None
    for (distance, count), piece in reversed(list(zip(doublings(pair_count), coarse_grads))):
        if far is not None:
            piece = piece.astype(jnp.float32) + far[distance : distance + count]
        piece = piece.astype(jnp.bfloat16)
        if distance == 1:
            relayed_back = after(relayed_back, piece)
            pair_total = pair_grad + relayed_back.astype(jnp.float32)
            pair_total = pair_total.astype(jnp.bfloat16)
        back = send(piece, shift_pairs(size, -distance))
        back = after(back, pair_total) if distance == 1 else back
        back = jnp.pad(back.astype(jnp.float32), [(0, distance - count)] + [(0, 0)] * 3)
        far = back if far is None else far[:distance] + back
    far = far[0]
    grad_back = send(pair_total, swap)
    other_far = send(far[:, block_rows:].astype(jnp.bfloat16), swap).astype(jnp.float32)
    out_back = after(out_back, piece)
    own_longer = lengthened(restrict, far[:, :block_rows])
    other_longer = lax.optimization_barrier(lengthened(restrict, other_far))
    home_total = home_grad + direct_back.astype(jnp.float32) + own_longer
    home_total = home_total.astype(jnp.bfloat16)

    def summed(n):
        other = grad_back[n].astype(jnp.float32) + other_longer[n]
        return whole(home_total[n], other.astype(jnp.bfloat16))

    return whole(out, out_back[0]), whole(grad_q, out_back[1]), summed(0), summed(1)


def solution(mesh):
    split = P(("prompt", "seq"), None)
    return jax.shard_map(
        per_device,
        mesh=mesh,
        in_specs=(split, split, split, split, P(), P()),
        out_specs=(split, split, split, split),
        check_vma=False,
    )
```

```python
import math

import jax
import jax.numpy as jnp
from jax import lax
from jax.experimental import pallas as pl
from jax.experimental.pallas import tpu as pltpu
from jax.sharding import PartitionSpec as P

HEAD_DIM = 64
PAIR = 2 * HEAD_DIM
TILE = 32
GRANT = 32 * 1024 * 1024

level_one_bias = math.log(32.0)
level_two_bias = math.log(64.0)
masked_bias = -1e30


def swap_pairs(size):
    return [(i, i ^ 1) for i in range(size)]


def direct_pairs(size):
    return [(i, j) for i in range(size) for j in [i + 2 if i % 2 else i - 2] if 0 <= j < size]


def inverse(pairs):
    return [(j, i) for i, j in pairs]


def shift_pairs(size, shift):
    return [(i, (i + 2 * shift) % size) for i in range(size)]


def dot(a, b):
    return jnp.dot(a, b, preferred_element_type=jnp.float32)


def block_diagonal(both):
    top, bottom = (both[:HEAD_DIM], both[HEAD_DIM:])
    zero = jnp.zeros_like(top)
    return jnp.concatenate(
        [jnp.concatenate([top, zero], axis=1), jnp.concatenate([zero, bottom], axis=1)], axis=0
    )


def stacked_heads(both):
    lane = lax.broadcasted_iota(jnp.int32, both.shape, 1)
    first = lane < HEAD_DIM
    zero = jnp.zeros_like(both)
    return jnp.concatenate([jnp.where(first, both, zero), jnp.where(first, zero, both)], axis=0)


def head_rows(both, h):
    return both[h * HEAD_DIM : (h + 1) * HEAD_DIM]


class Unit:
    def __init__(self, query, cotangent, keys, values, keys_t, values_t, bias):
        scaled = query.astype(jnp.float32) * (1.0 / math.sqrt(HEAD_DIM))
        scaled = scaled.astype(jnp.bfloat16)
        self.rows = query.shape[0]
        self.keys, self.values, self.keys_t, self.values_t = (keys, values, keys_t, values_t)
        self.bias = bias
        self.query_wide = block_diagonal(scaled.T)
        self.query_tall = stacked_heads(scaled)
        self.cotangent_t = cotangent.T.astype(jnp.float32)
        self.scores = {}
        self.highest = None
        self.total = 0.0
        self.weights = {}
        self.raw = [0.0, 0.0]
        self.grad_q_t = [0.0, 0.0]
        self.grads = []

    def columns(self, h):
        return slice(h * self.rows, (h + 1) * self.rows)

    def score(self, part):
        score = dot(self.keys[part], self.query_wide)
        plain = max(0, self.keys.shape[0] - self.bias.shape[0] - part.start)
        if plain < score.shape[0]:
            skip = part.start + plain - (self.keys.shape[0] - self.bias.shape[0])
            biased = score[plain:] + self.bias[skip : skip + score.shape[0] - plain]
            score = jnp.concatenate([score[:plain], biased], axis=0) if plain else biased
        highest = jnp.max(score, axis=0, keepdims=True)
        self.highest = highest if self.highest is None else jnp.maximum(self.highest, highest)
        self.scores[part.start] = score

    def weigh(self, part):
        score = self.scores[part.start]
        parts = []
        for start in range(0, score.shape[0], TILE):
            prob = jnp.exp(score[start : start + TILE] - self.highest)
            self.total = self.total + jnp.sum(prob.reshape(-1, 8, prob.shape[1]), axis=0)
            parts.append(prob.astype(jnp.bfloat16))
        weight = jnp.concatenate(parts, axis=0)
        for h in range(2):
            self.raw[h] = self.raw[h] + dot(
                head_rows(self.values_t, h)[:, part], weight[:, self.columns(h)]
            )
        self.weights[part.start] = weight

    def finish(self):
        share = 1.0 / jnp.sum(self.total, axis=0, keepdims=True)
        shares = [share[:, self.columns(h)] for h in range(2)]
        out_t = jnp.concatenate([self.raw[h] * shares[h] for h in range(2)], axis=0)
        out_t = out_t.astype(jnp.bfloat16)
        self.out = out_t.T
        product = self.cotangent_t * out_t.astype(jnp.float32)
        self.delta = jnp.concatenate(
            [
                jnp.sum(head_rows(product, h), axis=0, keepdims=True) * shares[h]
                for h in range(2)
            ],
            axis=1,
        )
        shared_t = jnp.concatenate(
            [head_rows(self.cotangent_t, h) * shares[h] for h in range(2)], axis=0
        )
        shared_t = shared_t.astype(jnp.bfloat16)
        self.cotangent_wide = block_diagonal(shared_t)
        self.cotangent_tall = stacked_heads(shared_t.T)

    def differentiate(self, part):
        weight = self.weights[part.start]
        dots = dot(self.values[part], self.cotangent_wide)
        parts = []
        for start in range(0, dots.shape[0], TILE):
            rows = slice(start, start + TILE)
            grad = weight[rows].astype(jnp.float32) * (dots[rows] - self.delta)
            parts.append(grad.astype(jnp.bfloat16))
        score_grad = jnp.concatenate(parts, axis=0)
        self.grads.append((dot(score_grad, self.query_tall), dot(weight, self.cotangent_tall)))
        for h in range(2):
            self.grad_q_t[h] = self.grad_q_t[h] + dot(
                head_rows(self.keys_t, h)[:, part], score_grad[:, self.columns(h)]
            )

    def grad_q(self):
        grad_q_t = jnp.concatenate(self.grad_q_t, axis=0) * (1.0 / math.sqrt(HEAD_DIM))
        return grad_q_t.astype(jnp.bfloat16).T

    def key_grad(self, n):
        return jnp.concatenate([grads[n] for grads in self.grads], axis=0)


def attention_kernel(shifts, one_rows, two_rows):
    def kernel(
        place, q, k, v, c, pair_k, pair_v, relayed_k, relayed_v, pair_qc, direct, pair_coarse, *rest
    ):
        coarse = rest[:shifts]
        out, grad_q, pair_out, home_grad, pair_grad, direct_grad, relayed_grad = rest[
            shifts : shifts + 7
        ]
        coarse_grads = rest[shifts + 7 :]
        rows = q.shape[0]

        parity, pair = (place[0], place[3])
        coarse_rows = pair_coarse.shape[2]

        def halo(have):
            return jnp.full((rows, 2 * rows), jnp.where(have > 0, 0.0, masked_bias), jnp.float32)

        def coarse_bias(query_block):
            row = lax.broadcasted_iota(jnp.int32, (coarse_rows, 2 * rows), 0)
            pieces = []
            for side in (parity, 1 - parity):
                for shift in range(1, shifts + 1):
                    sender = jnp.where(pair >= shift, pair - shift, pair - shift + shifts + 1)
                    apart = jnp.abs(2 * sender + side - query_block)
                    one = jnp.where((apart == 2) | (apart == 3), level_one_bias, masked_bias)
                    two = jnp.where(apart >= 4, level_two_bias, masked_bias)
                    rest = jnp.where(row < one_rows + two_rows, two, masked_bias)
                    pieces.append(jnp.where(row < one_rows, one, rest))
            return jnp.concatenate(pieces, axis=0).astype(jnp.float32)

        def chunk(pieces):
            return jnp.concatenate(pieces, axis=0), jnp.concatenate([a.T for a in pieces], axis=1)

        def shared(n, home, partner):
            far = [ref[0, n] for ref in coarse] + [pair_coarse[m, n] for m in range(shifts)]
            far = jnp.concatenate(far, axis=0)
            return chunk([home[...], partner[...]]), chunk([far])

        both_keys, both_values = (shared(0, k, pair_k), shared(1, v, pair_v))

        def key_rows(outer, near_far):
            near, far = near_far
            pieces = [near, chunk([outer]), far]
            return [jnp.concatenate([a[n] for a in pieces], axis=n) for n in range(2)]

        def unit(query, cotangent, outer_k, outer_v, have, bias):
            keys, keys_t = key_rows(outer_k, both_keys)
            values, values_t = key_rows(outer_v, both_values)
            bias = jnp.concatenate([halo(have), bias], axis=0)
            return Unit(query, cotangent, keys, values, keys_t, values_t, bias)

        one = unit(q[...], c[...], relayed_k[...], relayed_v[...], place[1], coarse_bias(2 * pair + parity))
        two = unit(pair_qc[0], pair_qc[1], direct[0], direct[1], place[2], coarse_bias(2 * pair + 1 - parity))
        count = one.keys.shape[0]
        parts = [slice(0, count)]
        for part in parts:
            one.score(part)
        for part in parts:
            two.score(part)
            one.weigh(part)
        one.finish()
        for part in parts:
            one.differentiate(part)
            two.weigh(part)
        two.finish()
        for part in parts:
            two.differentiate(part)
        out[...], grad_q[...] = (one.out, one.grad_q())
        pair_out[0], pair_out[1] = (two.out, two.grad_q())
        for n in range(2):
            first, second = (one.key_grad(n), two.key_grad(n))
            home_grad[n] = first[:rows] + second[:rows]
            pair_grad[n] = first[rows : 2 * rows] + second[rows : 2 * rows]
            relayed_grad[n] = first[2 * rows : 3 * rows].astype(relayed_grad.dtype)
            direct_grad[n] = second[2 * rows : 3 * rows].astype(direct_grad.dtype)
            far_grad = (first[3 * rows :] + second[3 * rows :]).astype(direct_grad.dtype)
            for m, ref in enumerate(coarse_grads):
                for side in range(2):
                    start = (side * shifts + m) * coarse_rows
                    piece = far_grad[start : start + coarse_rows]
                    ref[n, side * coarse_rows : (side + 1) * coarse_rows] = piece

    return kernel


def attention(
    place, level_rows, q, k, v, c, pair_k, pair_v, relayed_k, relayed_v, pair_qc, direct, pair_coarse, coarse
):
    rows, width = q.shape
    columns = width // 2
    steps = columns // PAIR
    shifts = len(coarse)
    coarse_rows = pair_coarse.shape[2]

    def mine(j, place):
        return place[0] * steps + j

    def flat(index):
        return pl.BlockSpec((rows, PAIR), index)

    def both(shape_rows):
        return pl.BlockSpec((2, shape_rows, PAIR), lambda j, place: (0, 0, j))

    key_count = 3 * rows + 2 * shifts * coarse_rows
    products = 6 * 2 * 2 * rows * key_count * HEAD_DIM * 2 * steps
    bf16, f32 = (jnp.bfloat16, jnp.float32)
    return pl.pallas_call(
        attention_kernel(shifts, *level_rows),
        grid_spec=pltpu.PrefetchScalarGridSpec(
            num_scalar_prefetch=1,
            grid=(steps,),
            in_specs=[flat(lambda j, place: (0, mine(j, place)))] * 4
            + [flat(lambda j, place: (0, j))] * 4
            + [both(rows)] * 2
            + [pl.BlockSpec((shifts, 2, coarse_rows, PAIR), lambda j, place: (0, 0, 0, j))]
            + [pl.BlockSpec((1, 2, coarse_rows, PAIR), lambda j, place: (place[0], 0, 0, j))]
            * shifts,
            out_specs=[flat(lambda j, place: (0, j))] * 2
            + [both(rows)] * 5
            + [both(2 * coarse_rows)] * shifts,
        ),
        out_shape=[jax.ShapeDtypeStruct((rows, columns), bf16)] * 2
        + [
            jax.ShapeDtypeStruct((2, rows, columns), bf16),
            jax.ShapeDtypeStruct((2, rows, columns), f32),
            jax.ShapeDtypeStruct((2, rows, columns), f32),
            jax.ShapeDtypeStruct((2, rows, columns), bf16),
            jax.ShapeDtypeStruct((2, rows, columns), bf16),
        ]
        + [jax.ShapeDtypeStruct((2, 2 * coarse_rows, columns), bf16)] * shifts,
        compiler_params=pltpu.CompilerParams(vmem_limit_bytes=GRANT),
        cost_estimate=pl.CostEstimate(
            flops=4 * products, bytes_accessed=40 * rows * columns, transcendentals=0
        ),
        name="attention",
    )(
        place, q, k, v, c, pair_k, pair_v, relayed_k, relayed_v, pair_qc, direct, pair_coarse, *coarse
    )


def restrict_kernel(restrict, k, v, out):
    half = out.shape[3]
    for n, ref in enumerate((k, v)):
        for side in range(2):
            columns = ref[:, side * half : (side + 1) * half]
            out[side, n] = dot(restrict[...], columns).astype(out.dtype)


def restricted(restrict, keys, values):
    vmem = pl.BlockSpec(memory_space=pltpu.VMEM)
    return pl.pallas_call(
        restrict_kernel,
        in_specs=[vmem] * 3,
        out_specs=vmem,
        out_shape=jax.ShapeDtypeStruct(
            (2, 2, restrict.shape[0], keys.shape[1] // 2), keys.dtype
        ),
        compiler_params=pltpu.CompilerParams(vmem_limit_bytes=GRANT),
        name="restrict",
    )(restrict, keys, values)


def lengthened(restrict, coarse):
    return jnp.einsum(
        "fb,nfc->nbc", restrict.astype(jnp.float32), coarse, precision=lax.Precision.HIGHEST
    )


def per_device(queries, keys, values, cotangent, restrict_one, restrict_two):
    rows, width = queries.shape
    size = lax.axis_size("seq")
    pair_count = size // 2
    position = lax.axis_index("seq")
    parity = lax.rem(position, 2)
    pair = lax.div(position, 2)
    one_rows, two_rows = (restrict_one.shape[0], restrict_two.shape[0])
    block_rows = -(-(one_rows + two_rows) // 16) * 16
    restrict = jnp.concatenate(
        [
            restrict_one,
            restrict_two,
            jnp.zeros((block_rows - one_rows - two_rows, rows), restrict_one.dtype),
        ],
        axis=0,
    )

    has_before, has_after = (pair > 0, pair < pair_count - 1)
    place = jnp.stack(
        [
            parity,
            jnp.where(parity == 0, has_before, has_after).astype(jnp.int32),
            jnp.where(parity == 0, has_after, has_before).astype(jnp.int32),
            pair,
        ]
    ).astype(jnp.int32)

    direct_to = direct_pairs(size)
    relayed_to = inverse(direct_to)
    swap = swap_pairs(size)

    def send(value, pairs):
        return lax.ppermute(value, "seq", pairs)

    half = width // 2
    shifts = range(1, pair_count)

    def columns(side, *arrays):
        return [lax.dynamic_slice_in_dim(a, side * half, half, axis=a.ndim - 1) for a in arrays]

    def after(value, *others):
        return lax.optimization_barrier((value, *others))[0]

    pair_k, pair_v = (send(a, swap) for a in columns(1 - parity, keys, values))
    own_coarse = after(restricted(restrict, keys, values), pair_k)
    coarse = [send(own_coarse, shift_pairs(size, s)) for s in shifts]
    relayed_k = send(pair_k, relayed_to)
    home_kv = jnp.stack(columns(parity, keys, values))
    direct = send(after(home_kv, pair_k), direct_to)
    sent_qc = jnp.stack(columns(1 - parity, queries, cotangent))
    pair_qc = send(after(sent_qc, pair_v), swap)
    relayed_v = send(after(pair_v, relayed_k), relayed_to)
    sent_coarse = jnp.concatenate(
        [lax.dynamic_slice_in_dim(a, 1 - parity, 1) for a in after(coarse, pair_v)], axis=0
    )
    pair_coarse = send(sent_coarse, swap)
    relayed_v = after(relayed_v, direct)
    pair_qc = after(pair_qc, relayed_v)

    (
        out, grad_q, pair_out, home_grad, pair_grad, direct_grad, relayed_grad, *coarse_grads,
    ) = attention(
        place, (one_rows, two_rows), queries, keys, values, cotangent,
        pair_k, pair_v, relayed_k, relayed_v, pair_qc, direct, pair_coarse, coarse,
    )

    def whole(own, other):
        axis = own.ndim - 1
        return jnp.where(
            parity == 0,
            jnp.concatenate([own, other], axis=axis),
            jnp.concatenate([other, own], axis=axis),
        )

    relayed_back = send(relayed_grad, direct_to)
    out_back = send(pair_out, swap)
    coarse_back = [send(a, shift_pairs(size, -s)) for s, a in zip(shifts, coarse_grads)]
    direct_back = send(direct_grad, relayed_to)
    pair_total = pair_grad + relayed_back.astype(jnp.float32)
    far = sum(piece.astype(jnp.float32) for piece in after(coarse_back, pair_total))
    pair_total = pair_total + lengthened(restrict, far[:, block_rows:])
    grad_back = send(pair_total.astype(jnp.bfloat16), swap)
    home_total = home_grad + direct_back.astype(jnp.float32)
    home_total = home_total + lengthened(restrict, far[:, :block_rows])
    home_total = home_total.astype(jnp.bfloat16)
    return (
        whole(out, out_back[0]),
        whole(grad_q, out_back[1]),
        whole(home_total[0], grad_back[0]),
        whole(home_total[1], grad_back[1]),
    )


def solution(mesh):
    split = P(("prompt", "seq"), None)
    return jax.shard_map(
        per_device,
        mesh=mesh,
        in_specs=(split, split, split, split, P(), P()),
        out_specs=(split, split, split, split),
        check_vma=False,
    )
```

```python
import math

import jax
import jax.numpy as jnp
from jax import lax
from jax.experimental import pallas as pl
from jax.experimental.pallas import tpu as pltpu
from jax.sharding import PartitionSpec as P

HEAD_DIM = 64
PAIR = 2 * HEAD_DIM
TILE = 32
GRANT = 16 * 1024 * 1024

level_one_bias = math.log(32.0)
level_two_bias = math.log(64.0)
masked_bias = -1e30


def swap_pairs(size):
    return [(i, i ^ 1) for i in range(size)]


def direct_pairs(size):
    return [(i, j) for i in range(size) for j in [i + 2 if i % 2 else i - 2] if 0 <= j < size]


def inverse(pairs):
    return [(j, i) for i, j in pairs]


def shift_pairs(size, shift):
    return [(i, (i + 2 * shift) % size) for i in range(size)]


def both_levels(shift, pair_count):
    return shift == 2 or shift == pair_count - 2


def dot(a, b):
    return jnp.dot(a, b, preferred_element_type=jnp.float32)


def block_diagonal(both):
    top, bottom = (both[:HEAD_DIM], both[HEAD_DIM:])
    zero = jnp.zeros_like(top)
    return jnp.concatenate(
        [jnp.concatenate([top, zero], axis=1), jnp.concatenate([zero, bottom], axis=1)], axis=0
    )


def stacked_heads(both):
    lane = lax.broadcasted_iota(jnp.int32, both.shape, 1)
    first = lane < HEAD_DIM
    zero = jnp.zeros_like(both)
    return jnp.concatenate([jnp.where(first, both, zero), jnp.where(first, zero, both)], axis=0)


def head_rows(both, h):
    return both[h * HEAD_DIM : (h + 1) * HEAD_DIM]


class Unit:
    def __init__(self, query, cotangent, keys, values, keys_t, values_t, bias):
        scaled = query.astype(jnp.float32) * (1.0 / math.sqrt(HEAD_DIM))
        scaled = scaled.astype(jnp.bfloat16)
        self.rows = query.shape[0]
        self.keys, self.values, self.keys_t, self.values_t = (keys, values, keys_t, values_t)
        self.bias = bias
        self.query_wide = block_diagonal(scaled.T)
        self.query_tall = stacked_heads(scaled)
        self.cotangent_t = cotangent.T.astype(jnp.float32)
        self.scores = {}
        self.highest = None
        self.total = 0.0
        self.weights = {}
        self.raw = [0.0, 0.0]
        self.grad_q_t = [0.0, 0.0]
        self.grads = []

    def columns(self, h):
        return slice(h * self.rows, (h + 1) * self.rows)

    def score(self, part):
        score = dot(self.keys[part], self.query_wide)
        plain = max(0, self.keys.shape[0] - self.bias.shape[0] - part.start)
        if plain < score.shape[0]:
            skip = part.start + plain - (self.keys.shape[0] - self.bias.shape[0])
            biased = score[plain:] + self.bias[skip : skip + score.shape[0] - plain]
            score = jnp.concatenate([score[:plain], biased], axis=0) if plain else biased
        highest = jnp.max(score, axis=0, keepdims=True)
        self.highest = highest if self.highest is None else jnp.maximum(self.highest, highest)
        self.scores[part.start] = score

    def weigh(self, part):
        score = self.scores[part.start]
        parts = []
        for start in range(0, score.shape[0], TILE):
            prob = jnp.exp(score[start : start + TILE] - self.highest)
            self.total = self.total + jnp.sum(prob.reshape(-1, 8, prob.shape[1]), axis=0)
            parts.append(prob.astype(jnp.bfloat16))
        weight = jnp.concatenate(parts, axis=0)
        for h in range(2):
            self.raw[h] = self.raw[h] + dot(
                head_rows(self.values_t, h)[:, part], weight[:, self.columns(h)]
            )
        self.weights[part.start] = weight

    def finish(self):
        share = 1.0 / jnp.sum(self.total, axis=0, keepdims=True)
        shares = [share[:, self.columns(h)] for h in range(2)]
        out_t = jnp.concatenate([self.raw[h] * shares[h] for h in range(2)], axis=0)
        out_t = out_t.astype(jnp.bfloat16)
        self.out = out_t.T
        product = self.cotangent_t * out_t.astype(jnp.float32)
        self.delta = jnp.concatenate(
            [
                jnp.sum(head_rows(product, h), axis=0, keepdims=True) * shares[h]
                for h in range(2)
            ],
            axis=1,
        )
        shared_t = jnp.concatenate(
            [head_rows(self.cotangent_t, h) * shares[h] for h in range(2)], axis=0
        )
        shared_t = shared_t.astype(jnp.bfloat16)
        self.cotangent_wide = block_diagonal(shared_t)
        self.cotangent_tall = stacked_heads(shared_t.T)

    def differentiate(self, part):
        weight = self.weights[part.start]
        dots = dot(self.values[part], self.cotangent_wide)
        parts = []
        for start in range(0, dots.shape[0], TILE):
            rows = slice(start, start + TILE)
            grad = weight[rows].astype(jnp.float32) * (dots[rows] - self.delta)
            parts.append(grad.astype(jnp.bfloat16))
        score_grad = jnp.concatenate(parts, axis=0)
        self.grads.append((dot(score_grad, self.query_tall), dot(weight, self.cotangent_tall)))
        for h in range(2):
            self.grad_q_t[h] = self.grad_q_t[h] + dot(
                head_rows(self.keys_t, h)[:, part], score_grad[:, self.columns(h)]
            )

    def grad_q(self):
        grad_q_t = jnp.concatenate(self.grad_q_t, axis=0) * (1.0 / math.sqrt(HEAD_DIM))
        return grad_q_t.astype(jnp.bfloat16).T

    def key_grad(self, n):
        return jnp.concatenate([grads[n] for grads in self.grads], axis=0)


def attention_kernel(shifts, one_rows, two_rows):
    def kernel(
        place, q, k, v, c, pair_k, pair_v, relayed_k, relayed_v, pair_qc, direct, pair_coarse, *rest
    ):
        coarse = rest[:shifts]
        out, grad_q, pair_out, home_grad, pair_grad, direct_grad, relayed_grad = rest[
            shifts : shifts + 7
        ]
        coarse_grads = rest[shifts + 7 :]
        rows = q.shape[0]

        parity, pair = (place[0], place[3])

        def halo(have):
            return jnp.full((rows, 2 * rows), jnp.where(have > 0, 0.0, masked_bias), jnp.float32)

        sizes = [ref.shape[2] for ref in coarse]
        starts = [sum(sizes[:m]) for m in range(shifts + 1)]

        def coarse_bias(query_block):
            pieces = []
            for side in (parity, 1 - parity):
                for shift, size in enumerate(sizes, start=1):
                    row = lax.broadcasted_iota(jnp.int32, (size, 2 * rows), 0)
                    sender = jnp.where(pair >= shift, pair - shift, pair - shift + shifts + 1)
                    apart = jnp.abs(2 * sender + side - query_block)
                    one = jnp.where((apart == 2) | (apart == 3), level_one_bias, masked_bias)
                    two = jnp.where(apart >= 4, level_two_bias, masked_bias)
                    if both_levels(shift, shifts + 1):
                        two = jnp.where(row < one_rows + two_rows, two, masked_bias)
                        pieces.append(jnp.where(row < one_rows, one, two))
                    else:
                        near = jnp.abs(sender - pair) == 1
                        one = jnp.where(near, one, masked_bias)
                        two = jnp.where(near, one, two)
                        one = jnp.where(row < one_rows, one, masked_bias)
                        pieces.append(jnp.where(row < two_rows, two, one))
            return jnp.concatenate(pieces, axis=0).astype(jnp.float32)

        def chunk(pieces):
            return jnp.concatenate(pieces, axis=0), jnp.concatenate([a.T for a in pieces], axis=1)

        def shared(n, home, partner):
            far = jnp.concatenate([ref[0, n].astype(jnp.float32) for ref in coarse], axis=0)
            far = jnp.concatenate([far.astype(jnp.bfloat16), pair_coarse[n]], axis=0)
            return chunk([home[...], partner[...]]), chunk([far])

        both_keys, both_values = (shared(0, k, pair_k), shared(1, v, pair_v))

        def key_rows(outer, near_far):
            near, far = near_far
            pieces = [near, chunk([outer]), far]
            return [jnp.concatenate([a[n] for a in pieces], axis=n) for n in range(2)]

        def unit(query, cotangent, outer_k, outer_v, have, bias):
            keys, keys_t = key_rows(outer_k, both_keys)
            values, values_t = key_rows(outer_v, both_values)
            bias = jnp.concatenate([halo(have), bias], axis=0)
            return Unit(query, cotangent, keys, values, keys_t, values_t, bias)

        one = unit(q[...], c[...], relayed_k[...], relayed_v[...], place[1], coarse_bias(2 * pair + parity))
        two = unit(pair_qc[0], pair_qc[1], direct[0], direct[1], place[2], coarse_bias(2 * pair + 1 - parity))
        count = one.keys.shape[0]
        parts = [slice(0, count)]
        for part in parts:
            one.score(part)
        for part in parts:
            two.score(part)
            one.weigh(part)
        one.finish()
        for part in parts:
            one.differentiate(part)
            two.weigh(part)
        two.finish()
        for part in parts:
            two.differentiate(part)
        out[...], grad_q[...] = (one.out, one.grad_q())
        pair_out[0], pair_out[1] = (two.out, two.grad_q())
        for n in range(2):
            first, second = (one.key_grad(n), two.key_grad(n))
            home_grad[n] = first[:rows] + second[:rows]
            pair_grad[n] = first[rows : 2 * rows] + second[rows : 2 * rows]
            relayed_grad[n] = first[2 * rows : 3 * rows].astype(relayed_grad.dtype)
            direct_grad[n] = second[2 * rows : 3 * rows].astype(direct_grad.dtype)
            far_grad = first[3 * rows :] + second[3 * rows :]
            for m, ref in enumerate(coarse_grads):
                cuts = [
                    slice(side * starts[-1] + starts[m], side * starts[-1] + starts[m + 1])
                    for side in range(2)
                ]
                piece = jnp.concatenate([far_grad[cut] for cut in cuts], axis=0)
                ref[n] = piece.astype(ref.dtype)

    return kernel


def attention(
    place, level_rows, q, k, v, c, pair_k, pair_v, relayed_k, relayed_v, pair_qc, direct, pair_coarse, coarse
):
    rows, width = q.shape
    columns = width // 2
    steps = columns // PAIR
    shifts = len(coarse)

    def mine(j, place):
        return place[0] * steps + j

    def flat(index):
        return pl.BlockSpec((rows, PAIR), index)

    def both(shape_rows):
        return pl.BlockSpec((2, shape_rows, PAIR), lambda j, place: (0, 0, j))

    key_count = 3 * rows + 2 * pair_coarse.shape[1]
    products = 6 * 2 * 2 * rows * key_count * HEAD_DIM * 2 * steps
    bf16, f32 = (jnp.bfloat16, jnp.float32)
    return pl.pallas_call(
        attention_kernel(shifts, *level_rows),
        grid_spec=pltpu.PrefetchScalarGridSpec(
            num_scalar_prefetch=1,
            grid=(steps,),
            in_specs=[flat(lambda j, place: (0, mine(j, place)))] * 4
            + [flat(lambda j, place: (0, j))] * 4
            + [both(rows)] * 2
            + [both(pair_coarse.shape[1])]
            + [
                pl.BlockSpec((1, 2, piece.shape[2], PAIR), lambda j, place: (place[0], 0, 0, j))
                for piece in coarse
            ],
            out_specs=[flat(lambda j, place: (0, j))] * 2
            + [both(rows)] * 5
            + [both(2 * piece.shape[2]) for piece in coarse],
        ),
        out_shape=[jax.ShapeDtypeStruct((rows, columns), bf16)] * 2
        + [
            jax.ShapeDtypeStruct((2, rows, columns), bf16),
            jax.ShapeDtypeStruct((2, rows, columns), f32),
            jax.ShapeDtypeStruct((2, rows, columns), f32),
            jax.ShapeDtypeStruct((2, rows, columns), bf16),
            jax.ShapeDtypeStruct((2, rows, columns), bf16),
        ]
        + [jax.ShapeDtypeStruct((2, 2 * piece.shape[2], columns), bf16) for piece in coarse],
        compiler_params=pltpu.CompilerParams(vmem_limit_bytes=GRANT),
        cost_estimate=pl.CostEstimate(
            flops=4 * products, bytes_accessed=40 * rows * columns, transcendentals=0
        ),
        name="attention",
    )(
        place, q, k, v, c, pair_k, pair_v, relayed_k, relayed_v, pair_qc, direct, pair_coarse, *coarse
    )


def restrict_kernel(place, restrict, k, v, spread, *outs):
    half = outs[0].shape[3]
    short = restrict.shape[0] // 2
    pair, shifts = (place[3], len(outs))

    def chosen(rows, shift):
        if both_levels(shift, shifts + 1):
            return rows
        apart = jnp.where(pair + shift <= shifts, shift, shifts + 1 - shift)
        return jnp.where(apart == 1, rows[:short], rows[short:])

    for n, ref in enumerate((k, v)):
        for side in range(2):
            rows = dot(restrict[...], ref[:, side * half : (side + 1) * half])
            for shift, out in enumerate(outs, start=1):
                out[side, n] = chosen(rows, shift).astype(out.dtype)
    whole = restrict[...].astype(jnp.float32)
    spread[...] = jnp.concatenate([chosen(whole, s) for s in range(1, shifts + 1)], axis=0)


def restricted(place, restrict, keys, values, pair_count):
    vmem = pl.BlockSpec(memory_space=pltpu.VMEM)
    rows = restrict.shape[0]
    sizes = [rows if both_levels(s, pair_count) else rows // 2 for s in range(1, pair_count)]
    return pl.pallas_call(
        restrict_kernel,
        in_specs=[pl.BlockSpec(memory_space=pltpu.SMEM)] + [vmem] * 3,
        out_specs=[vmem] * pair_count,
        out_shape=[jax.ShapeDtypeStruct((sum(sizes), restrict.shape[1]), jnp.float32)]
        + [jax.ShapeDtypeStruct((2, 2, size, keys.shape[1] // 2), keys.dtype) for size in sizes],
        compiler_params=pltpu.CompilerParams(vmem_limit_bytes=GRANT),
        name="restrict",
    )(place, restrict, keys, values)


def lengthened(restrict, coarse):
    return jnp.einsum(
        "fb,nfc->nbc", restrict, coarse, precision=lax.Precision.HIGHEST
    )


def per_device(queries, keys, values, cotangent, restrict_one, restrict_two):
    rows, width = queries.shape
    size = lax.axis_size("seq")
    pair_count = size // 2
    position = lax.axis_index("seq")
    parity = lax.rem(position, 2)
    pair = lax.div(position, 2)
    one_rows, two_rows = (restrict_one.shape[0], restrict_two.shape[0])
    short = max(one_rows, two_rows)
    block_rows = 2 * short
    restrict = jnp.concatenate(
        [
            jnp.pad(restrict_one, ((0, short - one_rows), (0, 0))),
            jnp.pad(restrict_two, ((0, short - two_rows), (0, 0))),
        ],
        axis=0,
    )

    has_before, has_after = (pair > 0, pair < pair_count - 1)
    place = jnp.stack(
        [
            parity,
            jnp.where(parity == 0, has_before, has_after).astype(jnp.int32),
            jnp.where(parity == 0, has_after, has_before).astype(jnp.int32),
            pair,
        ]
    ).astype(jnp.int32)

    direct_to = direct_pairs(size)
    relayed_to = inverse(direct_to)
    swap = swap_pairs(size)

    def send(value, pairs):
        return lax.ppermute(value, "seq", pairs)

    half = width // 2
    shifts = range(1, pair_count)

    def columns(side, *arrays):
        return [lax.dynamic_slice_in_dim(a, side * half, half, axis=a.ndim - 1) for a in arrays]

    def after(value, *others):
        return lax.optimization_barrier((value, *others))[0]

    pair_k, pair_v = (send(a, swap) for a in columns(1 - parity, keys, values))
    spread, *own_coarse = restricted(place, restrict, keys, values, pair_count)
    own_coarse = after(own_coarse, pair_k)
    coarse = [send(a, shift_pairs(size, s)) for s, a in zip(shifts, own_coarse)]
    relayed_k = send(pair_k, relayed_to)
    home_kv = jnp.stack(columns(parity, keys, values))
    direct = send(after(home_kv, coarse[0]), direct_to)
    sent_qc = jnp.stack(columns(1 - parity, queries, cotangent))
    pair_qc = send(after(sent_qc, pair_v), swap)
    relayed_v = send(after(pair_v, relayed_k), relayed_to)
    sent_coarse = jnp.concatenate(
        [
            lax.dynamic_slice_in_dim(a, 1 - parity, 1).reshape(a.shape[1:])
            for a in after(coarse, pair_v)
        ],
        axis=1,
    )
    pair_coarse = send(sent_coarse, swap)
    direct = after(direct, pair_qc)
    relayed_v = after(relayed_v, direct)

    (
        out, grad_q, pair_out, home_grad, pair_grad, direct_grad, relayed_grad, *coarse_grads,
    ) = attention(
        place, (one_rows, two_rows), queries, keys, values, cotangent,
        pair_k, pair_v, relayed_k, relayed_v, pair_qc, direct, pair_coarse, coarse,
    )

    def whole(own, other):
        axis = own.ndim - 1
        return jnp.where(
            parity == 0,
            jnp.concatenate([own, other], axis=axis),
            jnp.concatenate([other, own], axis=axis),
        )

    relayed_back = send(relayed_grad, direct_to)
    out_back = send(pair_out, swap)
    coarse_back = [send(a, shift_pairs(size, -s)) for s, a in zip(shifts, coarse_grads)]
    pair_total = pair_grad + relayed_back.astype(jnp.float32)
    far = [
        piece.astype(jnp.float32).reshape(2, 2, -1, half)
        for piece in after(coarse_back, pair_total)
    ]
    far = [jnp.concatenate([piece[:, side] for piece in far], axis=1) for side in range(2)]
    pair_total = pair_total + lengthened(spread, far[1])
    pair_total = pair_total.astype(jnp.bfloat16)
    grad_back = send(pair_total, swap)
    direct_back = send(after(direct_grad, pair_total), relayed_to)
    home_total = home_grad + direct_back.astype(jnp.float32)
    home_total = home_total + lengthened(spread, far[0])
    home_total = home_total.astype(jnp.bfloat16)
    return (
        whole(out, out_back[0]),
        whole(grad_q, out_back[1]),
        whole(home_total[0], grad_back[0]),
        whole(home_total[1], grad_back[1]),
    )


def solution(mesh):
    split = P(("prompt", "seq"), None)
    return jax.shard_map(
        per_device,
        mesh=mesh,
        in_specs=(split, split, split, split, P(), P()),
        out_specs=(split, split, split, split),
        check_vma=False,
    )
```

```python
import math

import jax
import jax.numpy as jnp
from jax import lax
from jax.experimental import pallas as pl
from jax.experimental.pallas import tpu as pltpu
from jax.sharding import PartitionSpec as P

HEAD_DIM = 64
PAIR = 2 * HEAD_DIM
TILE = 32
GRANT = 16 * 1024 * 1024

level_one_bias = math.log(32.0)
level_two_bias = math.log(64.0)
masked_bias = -1e30


def swap_pairs(size):
    return [(i, i ^ 1) for i in range(size)]


def direct_pairs(size):
    return [(i, j) for i in range(size) for j in [i + 2 if i % 2 else i - 2] if 0 <= j < size]


def inverse(pairs):
    return [(j, i) for i, j in pairs]


def shift_pairs(size, shift):
    return [(i, (i + 2 * shift) % size) for i in range(size)]


def both_levels(shift, pair_count):
    return shift == 2 or shift == pair_count - 2


def dot(a, b):
    return jnp.dot(a, b, preferred_element_type=jnp.float32)


def block_diagonal(both):
    top, bottom = (both[:HEAD_DIM], both[HEAD_DIM:])
    zero = jnp.zeros_like(top)
    return jnp.concatenate(
        [jnp.concatenate([top, zero], axis=1), jnp.concatenate([zero, bottom], axis=1)], axis=0
    )


def stacked_heads(both):
    lane = lax.broadcasted_iota(jnp.int32, both.shape, 1)
    first = lane < HEAD_DIM
    zero = jnp.zeros_like(both)
    return jnp.concatenate([jnp.where(first, both, zero), jnp.where(first, zero, both)], axis=0)


def head_rows(both, h):
    return both[h * HEAD_DIM : (h + 1) * HEAD_DIM]


class Unit:
    def __init__(self, query, cotangent, keys, values, keys_t, values_t, bias):
        scaled = query.astype(jnp.float32) * (1.0 / math.sqrt(HEAD_DIM))
        scaled = scaled.astype(jnp.bfloat16)
        self.rows = query.shape[0]
        self.keys, self.values, self.keys_t, self.values_t = (keys, values, keys_t, values_t)
        self.bias = bias
        self.query_wide = block_diagonal(scaled.T)
        self.query_tall = stacked_heads(scaled)
        self.cotangent_t = cotangent.T.astype(jnp.float32)
        self.scores = {}
        self.highest = None
        self.total = 0.0
        self.weights = {}
        self.raw = [0.0, 0.0]
        self.grad_q_t = [0.0, 0.0]
        self.grads = []

    def columns(self, h):
        return slice(h * self.rows, (h + 1) * self.rows)

    def score(self, part):
        score = dot(self.keys[part], self.query_wide)
        plain = max(0, self.keys.shape[0] - self.bias.shape[0] - part.start)
        if plain < score.shape[0]:
            skip = part.start + plain - (self.keys.shape[0] - self.bias.shape[0])
            biased = score[plain:] + self.bias[skip : skip + score.shape[0] - plain]
            score = jnp.concatenate([score[:plain], biased], axis=0) if plain else biased
        highest = jnp.max(score, axis=0, keepdims=True)
        self.highest = highest if self.highest is None else jnp.maximum(self.highest, highest)
        self.scores[part.start] = score

    def weigh(self, part):
        score = self.scores[part.start]
        parts = []
        for start in range(0, score.shape[0], TILE):
            prob = jnp.exp(score[start : start + TILE] - self.highest)
            self.total = self.total + jnp.sum(prob.reshape(-1, 8, prob.shape[1]), axis=0)
            parts.append(prob.astype(jnp.bfloat16))
        weight = jnp.concatenate(parts, axis=0)
        for h in range(2):
            self.raw[h] = self.raw[h] + dot(
                head_rows(self.values_t, h)[:, part], weight[:, self.columns(h)]
            )
        self.weights[part.start] = weight

    def finish(self):
        share = 1.0 / jnp.sum(self.total, axis=0, keepdims=True)
        shares = [share[:, self.columns(h)] for h in range(2)]
        out_t = jnp.concatenate([self.raw[h] * shares[h] for h in range(2)], axis=0)
        out_t = out_t.astype(jnp.bfloat16)
        self.out = out_t.T
        product = self.cotangent_t * out_t.astype(jnp.float32)
        self.delta = jnp.concatenate(
            [
                jnp.sum(head_rows(product, h), axis=0, keepdims=True) * shares[h]
                for h in range(2)
            ],
            axis=1,
        )
        shared_t = jnp.concatenate(
            [head_rows(self.cotangent_t, h) * shares[h] for h in range(2)], axis=0
        )
        shared_t = shared_t.astype(jnp.bfloat16)
        self.cotangent_wide = block_diagonal(shared_t)
        self.cotangent_tall = stacked_heads(shared_t.T)

    def differentiate(self, part):
        weight = self.weights[part.start]
        dots = dot(self.values[part], self.cotangent_wide)
        parts = []
        for start in range(0, dots.shape[0], TILE):
            rows = slice(start, start + TILE)
            grad = weight[rows].astype(jnp.float32) * (dots[rows] - self.delta)
            parts.append(grad.astype(jnp.bfloat16))
        score_grad = jnp.concatenate(parts, axis=0)
        self.grads.append((dot(score_grad, self.query_tall), dot(weight, self.cotangent_tall)))
        for h in range(2):
            self.grad_q_t[h] = self.grad_q_t[h] + dot(
                head_rows(self.keys_t, h)[:, part], score_grad[:, self.columns(h)]
            )

    def grad_q(self):
        grad_q_t = jnp.concatenate(self.grad_q_t, axis=0) * (1.0 / math.sqrt(HEAD_DIM))
        return grad_q_t.astype(jnp.bfloat16).T

    def key_grad(self, n):
        return jnp.concatenate([grads[n] for grads in self.grads], axis=0)


def attention_kernel(shifts, one_rows, two_rows):
    def kernel(
        place, q, k, v, c, pair_k, pair_v, relayed_k, relayed_v, pair_qc, direct, pair_coarse, *rest
    ):
        coarse = rest[:shifts]
        out, grad_q, pair_out, home_grad, pair_grad, direct_grad, relayed_grad = rest[
            shifts : shifts + 7
        ]
        coarse_grads = rest[shifts + 7 :]
        rows = q.shape[0]

        parity, pair = (place[0], place[3])

        def halo(have):
            return jnp.full((rows, 2 * rows), jnp.where(have > 0, 0.0, masked_bias), jnp.float32)

        sizes = [ref.shape[2] for ref in coarse]
        starts = [sum(sizes[:m]) for m in range(shifts + 1)]

        def coarse_bias(query_block):
            pieces = []
            for side in (parity, 1 - parity):
                for shift, size in enumerate(sizes, start=1):
                    row = lax.broadcasted_iota(jnp.int32, (size, 2 * rows), 0)
                    sender = jnp.where(pair >= shift, pair - shift, pair - shift + shifts + 1)
                    apart = jnp.abs(2 * sender + side - query_block)
                    one = jnp.where((apart == 2) | (apart == 3), level_one_bias, masked_bias)
                    two = jnp.where(apart >= 4, level_two_bias, masked_bias)
                    if both_levels(shift, shifts + 1):
                        two = jnp.where(row < one_rows + two_rows, two, masked_bias)
                        pieces.append(jnp.where(row < one_rows, one, two))
                    else:
                        near = jnp.abs(sender - pair) == 1
                        one = jnp.where(near, one, masked_bias)
                        two = jnp.where(near, one, two)
                        one = jnp.where(row < one_rows, one, masked_bias)
                        pieces.append(jnp.where(row < two_rows, two, one))
            return jnp.concatenate(pieces, axis=0).astype(jnp.float32)

        def chunk(pieces):
            return jnp.concatenate(pieces, axis=0), jnp.concatenate([a.T for a in pieces], axis=1)

        def shared(n, home, partner):
            far = jnp.concatenate([ref[0, n].astype(jnp.float32) for ref in coarse], axis=0)
            far = jnp.concatenate([far.astype(jnp.bfloat16), pair_coarse[n]], axis=0)
            return chunk([home[...], partner[...]]), chunk([far])

        both_keys, both_values = (shared(0, k, pair_k), shared(1, v, pair_v))

        def key_rows(outer, near_far):
            near, far = near_far
            pieces = [near, chunk([outer]), far]
            return [jnp.concatenate([a[n] for a in pieces], axis=n) for n in range(2)]

        def unit(query, cotangent, outer_k, outer_v, have, bias):
            keys, keys_t = key_rows(outer_k, both_keys)
            values, values_t = key_rows(outer_v, both_values)
            bias = jnp.concatenate([halo(have), bias], axis=0)
            return Unit(query, cotangent, keys, values, keys_t, values_t, bias)

        one = unit(q[...], c[...], relayed_k[...], relayed_v[...], place[1], coarse_bias(2 * pair + parity))
        two = unit(pair_qc[0], pair_qc[1], direct[0], direct[1], place[2], coarse_bias(2 * pair + 1 - parity))
        count = one.keys.shape[0]
        parts = [slice(0, count)]
        for part in parts:
            one.score(part)
        for part in parts:
            two.score(part)
            one.weigh(part)
        one.finish()
        for part in parts:
            one.differentiate(part)
            two.weigh(part)
        two.finish()
        for part in parts:
            two.differentiate(part)
        out[...], grad_q[...] = (one.out, one.grad_q())
        pair_out[0], pair_out[1] = (two.out, two.grad_q())
        for n in range(2):
            first, second = (one.key_grad(n), two.key_grad(n))
            home_grad[n] = first[:rows] + second[:rows]
            pair_grad[n] = first[rows : 2 * rows] + second[rows : 2 * rows]
            relayed_grad[n] = first[2 * rows : 3 * rows].astype(relayed_grad.dtype)
            direct_grad[n] = second[2 * rows : 3 * rows].astype(direct_grad.dtype)
            far_grad = first[3 * rows :] + second[3 * rows :]
            for m, ref in enumerate(coarse_grads):
                cuts = [
                    slice(side * starts[-1] + starts[m], side * starts[-1] + starts[m + 1])
                    for side in range(2)
                ]
                piece = jnp.concatenate([far_grad[cut] for cut in cuts], axis=0)
                ref[n] = piece.astype(ref.dtype)

    return kernel


def attention(
    place, level_rows, q, k, v, c, pair_k, pair_v, relayed_k, relayed_v, pair_qc, direct, pair_coarse, coarse
):
    rows, width = q.shape
    columns = width // 2
    steps = columns // PAIR
    shifts = len(coarse)

    def mine(j, place):
        return place[0] * steps + j

    def flat(index):
        return pl.BlockSpec((rows, PAIR), index)

    def both(shape_rows):
        return pl.BlockSpec((2, shape_rows, PAIR), lambda j, place: (0, 0, j))

    key_count = 3 * rows + 2 * pair_coarse.shape[1]
    products = 6 * 2 * 2 * rows * key_count * HEAD_DIM * 2 * steps
    bf16, f32 = (jnp.bfloat16, jnp.float32)
    return pl.pallas_call(
        attention_kernel(shifts, *level_rows),
        grid_spec=pltpu.PrefetchScalarGridSpec(
            num_scalar_prefetch=1,
            grid=(steps,),
            in_specs=[flat(lambda j, place: (0, mine(j, place)))] * 4
            + [flat(lambda j, place: (0, j))] * 4
            + [both(rows)] * 2
            + [both(pair_coarse.shape[1])]
            + [
                pl.BlockSpec((1, 2, piece.shape[2], PAIR), lambda j, place: (place[0], 0, 0, j))
                for piece in coarse
            ],
            out_specs=[flat(lambda j, place: (0, j))] * 2
            + [both(rows)] * 5
            + [both(2 * piece.shape[2]) for piece in coarse],
        ),
        out_shape=[jax.ShapeDtypeStruct((rows, columns), bf16)] * 2
        + [
            jax.ShapeDtypeStruct((2, rows, columns), bf16),
            jax.ShapeDtypeStruct((2, rows, columns), f32),
            jax.ShapeDtypeStruct((2, rows, columns), f32),
            jax.ShapeDtypeStruct((2, rows, columns), bf16),
            jax.ShapeDtypeStruct((2, rows, columns), bf16),
        ]
        + [jax.ShapeDtypeStruct((2, 2 * piece.shape[2], columns), bf16) for piece in coarse],
        compiler_params=pltpu.CompilerParams(vmem_limit_bytes=GRANT),
        cost_estimate=pl.CostEstimate(
            flops=4 * products, bytes_accessed=40 * rows * columns, transcendentals=0
        ),
        name="attention",
    )(
        place, q, k, v, c, pair_k, pair_v, relayed_k, relayed_v, pair_qc, direct, pair_coarse, *coarse
    )


def restrict_kernel(place, restrict, k, v, spread, *outs):
    half = outs[0].shape[3]
    short = restrict.shape[0] // 2
    pair, shifts = (place[3], len(outs))

    def chosen(rows, shift):
        if both_levels(shift, shifts + 1):
            return rows
        apart = jnp.where(pair + shift <= shifts, shift, shifts + 1 - shift)
        return jnp.where(apart == 1, rows[:short], rows[short:])

    for n, ref in enumerate((k, v)):
        for side in range(2):
            rows = dot(restrict[...], ref[:, side * half : (side + 1) * half])
            for shift, out in enumerate(outs, start=1):
                out[side, n] = chosen(rows, shift).astype(out.dtype)
    whole = restrict[...].astype(jnp.float32)
    spread[...] = jnp.concatenate([chosen(whole, s) for s in range(1, shifts + 1)], axis=0)


def restricted(place, restrict, keys, values, pair_count):
    vmem = pl.BlockSpec(memory_space=pltpu.VMEM)
    rows = restrict.shape[0]
    sizes = [rows if both_levels(s, pair_count) else rows // 2 for s in range(1, pair_count)]
    return pl.pallas_call(
        restrict_kernel,
        in_specs=[pl.BlockSpec(memory_space=pltpu.SMEM)] + [vmem] * 3,
        out_specs=[vmem] * pair_count,
        out_shape=[jax.ShapeDtypeStruct((sum(sizes), restrict.shape[1]), jnp.float32)]
        + [jax.ShapeDtypeStruct((2, 2, size, keys.shape[1] // 2), keys.dtype) for size in sizes],
        compiler_params=pltpu.CompilerParams(vmem_limit_bytes=GRANT),
        name="restrict",
    )(place, restrict, keys, values)


def lengthened(restrict, coarse):
    return jnp.einsum(
        "fb,nfc->nbc", restrict, coarse, precision=lax.Precision.HIGHEST
    )


def per_device(queries, keys, values, cotangent, restrict_one, restrict_two):
    rows, width = queries.shape
    size = lax.axis_size("seq")
    pair_count = size // 2
    position = lax.axis_index("seq")
    parity = lax.rem(position, 2)
    pair = lax.div(position, 2)
    one_rows, two_rows = (restrict_one.shape[0], restrict_two.shape[0])
    short = max(one_rows, two_rows)
    block_rows = 2 * short
    restrict = jnp.concatenate(
        [
            jnp.pad(restrict_one, ((0, short - one_rows), (0, 0))),
            jnp.pad(restrict_two, ((0, short - two_rows), (0, 0))),
        ],
        axis=0,
    )

    has_before, has_after = (pair > 0, pair < pair_count - 1)
    place = jnp.stack(
        [
            parity,
            jnp.where(parity == 0, has_before, has_after).astype(jnp.int32),
            jnp.where(parity == 0, has_after, has_before).astype(jnp.int32),
            pair,
        ]
    ).astype(jnp.int32)

    direct_to = direct_pairs(size)
    relayed_to = inverse(direct_to)
    swap = swap_pairs(size)

    def send(value, pairs):
        return lax.ppermute(value, "seq", pairs)

    half = width // 2
    shifts = range(1, pair_count)

    def columns(side, *arrays):
        return [lax.dynamic_slice_in_dim(a, side * half, half, axis=a.ndim - 1) for a in arrays]

    def after(value, *others):
        return lax.optimization_barrier((value, *others))[0]

    pair_k, pair_v = (send(a, swap) for a in columns(1 - parity, keys, values))
    spread, *own_coarse = restricted(place, restrict, keys, values, pair_count)
    own_coarse = after(own_coarse, pair_k)
    coarse = [send(a, shift_pairs(size, s)) for s, a in zip(shifts, own_coarse)]
    relayed_k = send(pair_k, relayed_to)
    home_kv = jnp.stack(columns(parity, keys, values))
    direct = send(after(home_kv, coarse[0]), direct_to)
    sent_qc = jnp.stack(columns(1 - parity, queries, cotangent))
    pair_qc = send(after(sent_qc, pair_v), swap)
    relayed_v = send(after(pair_v, relayed_k), relayed_to)
    sent_coarse = jnp.concatenate(
        [
            lax.dynamic_slice_in_dim(a, 1 - parity, 1).reshape(a.shape[1:])
            for a in after(coarse, pair_v)
        ],
        axis=1,
    )
    pair_coarse = send(sent_coarse, swap)
    direct = after(direct, pair_qc)
    relayed_v = after(relayed_v, direct)

    (
        out, grad_q, pair_out, home_grad, pair_grad, direct_grad, relayed_grad, *coarse_grads,
    ) = attention(
        place, (one_rows, two_rows), queries, keys, values, cotangent,
        pair_k, pair_v, relayed_k, relayed_v, pair_qc, direct, pair_coarse, coarse,
    )

    def whole(own, other):
        axis = own.ndim - 1
        return jnp.where(
            parity == 0,
            jnp.concatenate([own, other], axis=axis),
            jnp.concatenate([other, own], axis=axis),
        )

    relayed_back = send(relayed_grad, direct_to)
    out_back = send(pair_out, swap)
    pair_total = (pair_grad + relayed_back.astype(jnp.float32)).astype(jnp.bfloat16)
    grad_back = send(pair_total, swap)
    coarse_grads[-1] = after(coarse_grads[-1], pair_total)
    coarse_back = [send(a, shift_pairs(size, -s)) for s, a in zip(shifts, coarse_grads)]
    direct_back = send(direct_grad, relayed_to)
    far = [
        piece.astype(jnp.float32).reshape(2, 2, -1, half)
        for piece in after(coarse_back, pair_total)
    ]
    far = [jnp.concatenate([piece[:, side] for piece in far], axis=1) for side in range(2)]
    sent_far = far[1].astype(jnp.bfloat16)
    other_far = send(sent_far, swap).astype(jnp.float32)
    other_longer = lax.optimization_barrier(lengthened(spread, other_far))
    home_total = home_grad + direct_back.astype(jnp.float32)
    home_total = (home_total + lengthened(spread, far[0])).astype(jnp.bfloat16)
    pair_back = (grad_back.astype(jnp.float32) + other_longer).astype(jnp.bfloat16)
    return (
        whole(out, out_back[0]),
        whole(grad_q, out_back[1]),
        whole(home_total[0], pair_back[0]),
        whole(home_total[1], pair_back[1]),
    )


def solution(mesh):
    split = P(("prompt", "seq"), None)
    return jax.shard_map(
        per_device,
        mesh=mesh,
        in_specs=(split, split, split, split, P(), P()),
        out_specs=(split, split, split, split),
        check_vma=False,
    )
```

```python
import math

import jax
import jax.numpy as jnp
from jax import lax
from jax.experimental import pallas as pl
from jax.experimental.pallas import tpu as pltpu
from jax.sharding import PartitionSpec as P

HEAD_DIM = 64
PAIR = 2 * HEAD_DIM
TILE = 32
GRANT = 16 * 1024 * 1024

level_one_bias = math.log(32.0)
level_two_bias = math.log(64.0)
masked_bias = -1e30


def swap_pairs(size):
    return [(i, i ^ 1) for i in range(size)]


def direct_pairs(size):
    return [(i, j) for i in range(size) for j in [i + 2 if i % 2 else i - 2] if 0 <= j < size]


def inverse(pairs):
    return [(j, i) for i, j in pairs]


def shift_pairs(size, shift):
    return [(i, (i + 2 * shift) % size) for i in range(size)]


def both_levels(shift, pair_count):
    return shift == 2 or shift == pair_count - 2


def dot(a, b):
    return jnp.dot(a, b, preferred_element_type=jnp.float32)


def block_diagonal(both):
    top, bottom = (both[:HEAD_DIM], both[HEAD_DIM:])
    zero = jnp.zeros_like(top)
    return jnp.concatenate(
        [jnp.concatenate([top, zero], axis=1), jnp.concatenate([zero, bottom], axis=1)], axis=0
    )


def stacked_heads(both):
    lane = lax.broadcasted_iota(jnp.int32, both.shape, 1)
    first = lane < HEAD_DIM
    zero = jnp.zeros_like(both)
    return jnp.concatenate([jnp.where(first, both, zero), jnp.where(first, zero, both)], axis=0)


def head_rows(both, h):
    return both[h * HEAD_DIM : (h + 1) * HEAD_DIM]


class Unit:
    def __init__(self, query, cotangent, keys, values, keys_t, values_t, bias):
        scaled = query.astype(jnp.float32) * (1.0 / math.sqrt(HEAD_DIM))
        scaled = scaled.astype(jnp.bfloat16)
        self.rows = query.shape[0]
        self.keys, self.values, self.keys_t, self.values_t = (keys, values, keys_t, values_t)
        self.bias = bias
        self.query_wide = block_diagonal(scaled.T)
        self.query_tall = stacked_heads(scaled)
        self.cotangent_t = cotangent.T.astype(jnp.float32)
        self.scores = {}
        self.highest = None
        self.total = 0.0
        self.weights = {}
        self.raw = [0.0, 0.0]
        self.grad_q_t = [0.0, 0.0]
        self.grads = []

    def columns(self, h):
        return slice(h * self.rows, (h + 1) * self.rows)

    def score(self, part):
        score = dot(self.keys[part], self.query_wide)
        plain = max(0, self.keys.shape[0] - self.bias.shape[0] - part.start)
        if plain < score.shape[0]:
            skip = part.start + plain - (self.keys.shape[0] - self.bias.shape[0])
            biased = score[plain:] + self.bias[skip : skip + score.shape[0] - plain]
            score = jnp.concatenate([score[:plain], biased], axis=0) if plain else biased
        highest = jnp.max(score, axis=0, keepdims=True)
        self.highest = highest if self.highest is None else jnp.maximum(self.highest, highest)
        self.scores[part.start] = score

    def weigh(self, part):
        score = self.scores[part.start]
        parts = []
        for start in range(0, score.shape[0], TILE):
            prob = jnp.exp(score[start : start + TILE] - self.highest)
            self.total = self.total + jnp.sum(prob.reshape(-1, 8, prob.shape[1]), axis=0)
            parts.append(prob.astype(jnp.bfloat16))
        weight = jnp.concatenate(parts, axis=0)
        for h in range(2):
            self.raw[h] = self.raw[h] + dot(
                head_rows(self.values_t, h)[:, part], weight[:, self.columns(h)]
            )
        self.weights[part.start] = weight

    def finish(self):
        share = 1.0 / jnp.sum(self.total, axis=0, keepdims=True)
        shares = [share[:, self.columns(h)] for h in range(2)]
        out_t = jnp.concatenate([self.raw[h] * shares[h] for h in range(2)], axis=0)
        out_t = out_t.astype(jnp.bfloat16)
        self.out = out_t.T
        product = self.cotangent_t * out_t.astype(jnp.float32)
        self.delta = jnp.concatenate(
            [
                jnp.sum(head_rows(product, h), axis=0, keepdims=True) * shares[h]
                for h in range(2)
            ],
            axis=1,
        )
        shared_t = jnp.concatenate(
            [head_rows(self.cotangent_t, h) * shares[h] for h in range(2)], axis=0
        )
        shared_t = shared_t.astype(jnp.bfloat16)
        self.cotangent_wide = block_diagonal(shared_t)
        self.cotangent_tall = stacked_heads(shared_t.T)

    def differentiate(self, part):
        weight = self.weights[part.start]
        dots = dot(self.values[part], self.cotangent_wide)
        parts = []
        for start in range(0, dots.shape[0], TILE):
            rows = slice(start, start + TILE)
            grad = weight[rows].astype(jnp.float32) * (dots[rows] - self.delta)
            parts.append(grad.astype(jnp.bfloat16))
        score_grad = jnp.concatenate(parts, axis=0)
        self.grads.append((dot(score_grad, self.query_tall), dot(weight, self.cotangent_tall)))
        for h in range(2):
            self.grad_q_t[h] = self.grad_q_t[h] + dot(
                head_rows(self.keys_t, h)[:, part], score_grad[:, self.columns(h)]
            )

    def grad_q(self):
        grad_q_t = jnp.concatenate(self.grad_q_t, axis=0) * (1.0 / math.sqrt(HEAD_DIM))
        return grad_q_t.astype(jnp.bfloat16).T

    def key_grad(self, n):
        return jnp.concatenate([grads[n] for grads in self.grads], axis=0)


def attention_kernel(shifts, one_rows, two_rows):
    def kernel(
        place, q, k, v, c, pair_k, pair_v, relayed_k, relayed_v, pair_qc, direct, pair_coarse, *rest
    ):
        coarse = rest[:shifts]
        out, grad_q, pair_out, home_grad, pair_grad, direct_grad, relayed_grad = rest[
            shifts : shifts + 7
        ]
        coarse_grads = rest[shifts + 7 :]
        rows = q.shape[0]

        parity, pair = (place[0], place[3])

        def halo(have):
            return jnp.full((rows, 2 * rows), jnp.where(have > 0, 0.0, masked_bias), jnp.float32)

        sizes = [ref.shape[2] for ref in coarse]
        starts = [sum(sizes[:m]) for m in range(shifts + 1)]

        def coarse_bias(query_block):
            pieces = []
            for side in (parity, 1 - parity):
                for shift, size in enumerate(sizes, start=1):
                    row = lax.broadcasted_iota(jnp.int32, (size, 2 * rows), 0)
                    sender = jnp.where(pair >= shift, pair - shift, pair - shift + shifts + 1)
                    apart = jnp.abs(2 * sender + side - query_block)
                    one = jnp.where((apart == 2) | (apart == 3), level_one_bias, masked_bias)
                    two = jnp.where(apart >= 4, level_two_bias, masked_bias)
                    if both_levels(shift, shifts + 1):
                        two = jnp.where(row < one_rows + two_rows, two, masked_bias)
                        pieces.append(jnp.where(row < one_rows, one, two))
                    else:
                        near = jnp.abs(sender - pair) == 1
                        one = jnp.where(near, one, masked_bias)
                        two = jnp.where(near, one, two)
                        one = jnp.where(row < one_rows, one, masked_bias)
                        pieces.append(jnp.where(row < two_rows, two, one))
            return jnp.concatenate(pieces, axis=0).astype(jnp.float32)

        def chunk(pieces):
            return jnp.concatenate(pieces, axis=0), jnp.concatenate([a.T for a in pieces], axis=1)

        def shared(n, home, partner):
            far = jnp.concatenate([ref[0, n].astype(jnp.float32) for ref in coarse], axis=0)
            far = jnp.concatenate([far.astype(jnp.bfloat16), pair_coarse[n]], axis=0)
            return chunk([home[...], partner[...]]), chunk([far])

        both_keys, both_values = (shared(0, k, pair_k), shared(1, v, pair_v))

        def key_rows(outer, near_far):
            near, far = near_far
            pieces = [near, chunk([outer]), far]
            return [jnp.concatenate([a[n] for a in pieces], axis=n) for n in range(2)]

        def unit(query, cotangent, outer_k, outer_v, have, bias):
            keys, keys_t = key_rows(outer_k, both_keys)
            values, values_t = key_rows(outer_v, both_values)
            bias = jnp.concatenate([halo(have), bias], axis=0)
            return Unit(query, cotangent, keys, values, keys_t, values_t, bias)

        one = unit(q[...], c[...], relayed_k[...], relayed_v[...], place[1], coarse_bias(2 * pair + parity))
        two = unit(pair_qc[0], pair_qc[1], direct[0], direct[1], place[2], coarse_bias(2 * pair + 1 - parity))
        count = one.keys.shape[0]
        parts = [slice(0, count)]
        for part in parts:
            one.score(part)
        for part in parts:
            two.score(part)
            one.weigh(part)
        one.finish()
        for part in parts:
            one.differentiate(part)
            two.weigh(part)
        two.finish()
        for part in parts:
            two.differentiate(part)
        out[...], grad_q[...] = (one.out, one.grad_q())
        pair_out[0], pair_out[1] = (two.out, two.grad_q())
        for n in range(2):
            first, second = (one.key_grad(n), two.key_grad(n))
            home_grad[n] = first[:rows] + second[:rows]
            pair_grad[n] = first[rows : 2 * rows] + second[rows : 2 * rows]
            relayed_grad[n] = first[2 * rows : 3 * rows].astype(relayed_grad.dtype)
            direct_grad[n] = second[2 * rows : 3 * rows].astype(direct_grad.dtype)
            far_grad = first[3 * rows :] + second[3 * rows :]
            for m, ref in enumerate(coarse_grads):
                cuts = [
                    slice(side * starts[-1] + starts[m], side * starts[-1] + starts[m + 1])
                    for side in range(2)
                ]
                piece = jnp.concatenate([far_grad[cut] for cut in cuts], axis=0)
                ref[n] = piece.astype(ref.dtype)

    return kernel


def attention(
    place, level_rows, q, k, v, c, pair_k, pair_v, relayed_k, relayed_v, pair_qc, direct, pair_coarse, coarse
):
    rows, width = q.shape
    columns = width // 2
    steps = columns // PAIR
    shifts = len(coarse)

    def mine(j, place):
        return place[0] * steps + j

    def flat(index):
        return pl.BlockSpec((rows, PAIR), index)

    def both(shape_rows):
        return pl.BlockSpec((2, shape_rows, PAIR), lambda j, place: (0, 0, j))

    key_count = 3 * rows + 2 * pair_coarse.shape[1]
    products = 6 * 2 * 2 * rows * key_count * HEAD_DIM * 2 * steps
    bf16, f32 = (jnp.bfloat16, jnp.float32)
    return pl.pallas_call(
        attention_kernel(shifts, *level_rows),
        grid_spec=pltpu.PrefetchScalarGridSpec(
            num_scalar_prefetch=1,
            grid=(steps,),
            in_specs=[flat(lambda j, place: (0, mine(j, place)))] * 4
            + [flat(lambda j, place: (0, j))] * 4
            + [both(rows)] * 2
            + [both(pair_coarse.shape[1])]
            + [
                pl.BlockSpec((1, 2, piece.shape[2], PAIR), lambda j, place: (place[0], 0, 0, j))
                for piece in coarse
            ],
            out_specs=[flat(lambda j, place: (0, j))] * 2
            + [both(rows)] * 5
            + [both(2 * piece.shape[2]) for piece in coarse],
        ),
        out_shape=[jax.ShapeDtypeStruct((rows, columns), bf16)] * 2
        + [
            jax.ShapeDtypeStruct((2, rows, columns), bf16),
            jax.ShapeDtypeStruct((2, rows, columns), f32),
            jax.ShapeDtypeStruct((2, rows, columns), f32),
            jax.ShapeDtypeStruct((2, rows, columns), bf16),
            jax.ShapeDtypeStruct((2, rows, columns), bf16),
        ]
        + [jax.ShapeDtypeStruct((2, 2 * piece.shape[2], columns), bf16) for piece in coarse],
        compiler_params=pltpu.CompilerParams(vmem_limit_bytes=GRANT),
        cost_estimate=pl.CostEstimate(
            flops=4 * products, bytes_accessed=40 * rows * columns, transcendentals=0
        ),
        name="attention",
    )(
        place, q, k, v, c, pair_k, pair_v, relayed_k, relayed_v, pair_qc, direct, pair_coarse, *coarse
    )


def restrict_kernel(place, restrict, k, v, spread, *outs):
    half = outs[0].shape[3]
    short = restrict.shape[0] // 2
    pair, shifts = (place[3], len(outs))

    def chosen(rows, shift):
        if both_levels(shift, shifts + 1):
            return rows
        apart = jnp.where(pair + shift <= shifts, shift, shifts + 1 - shift)
        return jnp.where(apart == 1, rows[:short], rows[short:])

    for n, ref in enumerate((k, v)):
        for side in range(2):
            rows = dot(restrict[...], ref[:, side * half : (side + 1) * half])
            for shift, out in enumerate(outs, start=1):
                out[side, n] = chosen(rows, shift).astype(out.dtype)
    whole = restrict[...].astype(jnp.float32)
    spread[...] = jnp.concatenate([chosen(whole, s) for s in range(1, shifts + 1)], axis=0)


def restricted(place, restrict, keys, values, pair_count):
    vmem = pl.BlockSpec(memory_space=pltpu.VMEM)
    rows = restrict.shape[0]
    sizes = [rows if both_levels(s, pair_count) else rows // 2 for s in range(1, pair_count)]
    return pl.pallas_call(
        restrict_kernel,
        in_specs=[pl.BlockSpec(memory_space=pltpu.SMEM)] + [vmem] * 3,
        out_specs=[vmem] * pair_count,
        out_shape=[jax.ShapeDtypeStruct((sum(sizes), restrict.shape[1]), jnp.float32)]
        + [jax.ShapeDtypeStruct((2, 2, size, keys.shape[1] // 2), keys.dtype) for size in sizes],
        compiler_params=pltpu.CompilerParams(vmem_limit_bytes=GRANT),
        name="restrict",
    )(place, restrict, keys, values)


def lengthened(restrict, coarse):
    return jnp.einsum(
        "fb,nfc->nbc", restrict, coarse, precision=lax.Precision.HIGHEST
    )


def per_device(queries, keys, values, cotangent, restrict_one, restrict_two):
    rows, width = queries.shape
    size = lax.axis_size("seq")
    pair_count = size // 2
    position = lax.axis_index("seq")
    parity = lax.rem(position, 2)
    pair = lax.div(position, 2)
    one_rows, two_rows = (restrict_one.shape[0], restrict_two.shape[0])
    short = max(one_rows, two_rows)
    block_rows = 2 * short
    restrict = jnp.concatenate(
        [
            jnp.pad(restrict_one, ((0, short - one_rows), (0, 0))),
            jnp.pad(restrict_two, ((0, short - two_rows), (0, 0))),
        ],
        axis=0,
    )

    has_before, has_after = (pair > 0, pair < pair_count - 1)
    place = jnp.stack(
        [
            parity,
            jnp.where(parity == 0, has_before, has_after).astype(jnp.int32),
            jnp.where(parity == 0, has_after, has_before).astype(jnp.int32),
            pair,
        ]
    ).astype(jnp.int32)

    direct_to = direct_pairs(size)
    relayed_to = inverse(direct_to)
    swap = swap_pairs(size)

    def send(value, pairs):
        return lax.ppermute(value, "seq", pairs)

    half = width // 2
    shifts = range(1, pair_count)

    def columns(side, *arrays):
        return [lax.dynamic_slice_in_dim(a, side * half, half, axis=a.ndim - 1) for a in arrays]

    def after(value, *others):
        return lax.optimization_barrier((value, *others))[0]

    pair_k, pair_v = (send(a, swap) for a in columns(1 - parity, keys, values))
    spread, *own_coarse = restricted(place, restrict, keys, values, pair_count)
    own_coarse = after(own_coarse, pair_k)
    coarse = [send(a, shift_pairs(size, s)) for s, a in zip(shifts, own_coarse)]
    relayed_k = send(pair_k, relayed_to)
    home_kv = jnp.stack(columns(parity, keys, values))
    direct = send(after(home_kv, coarse[0]), direct_to)
    sent_qc = jnp.stack(columns(1 - parity, queries, cotangent))
    pair_qc = send(after(sent_qc, pair_v), swap)
    relayed_v = send(after(pair_v, relayed_k), relayed_to)
    sent_coarse = jnp.concatenate(
        [
            lax.dynamic_slice_in_dim(a, 1 - parity, 1).reshape(a.shape[1:])
            for a in after(coarse, pair_v)
        ],
        axis=1,
    )
    pair_coarse = send(sent_coarse, swap)
    direct = after(direct, pair_qc)
    relayed_v = after(relayed_v, direct)

    (
        out, grad_q, pair_out, home_grad, pair_grad, direct_grad, relayed_grad, *coarse_grads,
    ) = attention(
        place, (one_rows, two_rows), queries, keys, values, cotangent,
        pair_k, pair_v, relayed_k, relayed_v, pair_qc, direct, pair_coarse, coarse,
    )

    def whole(own, other):
        axis = own.ndim - 1
        return jnp.where(
            parity == 0,
            jnp.concatenate([own, other], axis=axis),
            jnp.concatenate([other, own], axis=axis),
        )

    relayed_back = send(relayed_grad, direct_to)
    out_back = send(pair_out, swap)
    coarse_back = [send(a, shift_pairs(size, -s)) for s, a in zip(shifts, coarse_grads)]
    pair_total = (pair_grad + relayed_back.astype(jnp.float32)).astype(jnp.bfloat16)
    grad_back = send(pair_total, swap)
    direct_back = send(after(direct_grad, pair_total), relayed_to)
    far = [
        piece.astype(jnp.float32).reshape(2, 2, -1, half)
        for piece in after(coarse_back, pair_total)
    ]
    far = [jnp.concatenate([piece[:, side] for piece in far], axis=1) for side in range(2)]
    sent_far = far[1].astype(jnp.bfloat16)
    other_far = send(sent_far, swap).astype(jnp.float32)
    other_longer = lax.optimization_barrier(lengthened(spread, other_far))
    home_total = home_grad + direct_back.astype(jnp.float32)
    home_total = (home_total + lengthened(spread, far[0])).astype(jnp.bfloat16)
    pair_back = (grad_back.astype(jnp.float32) + other_longer).astype(jnp.bfloat16)
    return (
        whole(out, out_back[0]),
        whole(grad_q, out_back[1]),
        whole(home_total[0], pair_back[0]),
        whole(home_total[1], pair_back[1]),
    )


def solution(mesh):
    split = P(("prompt", "seq"), None)
    return jax.shard_map(
        per_device,
        mesh=mesh,
        in_specs=(split, split, split, split, P(), P()),
        out_specs=(split, split, split, split),
        check_vma=False,
    )
```

```python
import math

import jax
import jax.numpy as jnp
from jax import lax
from jax.experimental import pallas as pl
from jax.experimental.pallas import tpu as pltpu
from jax.sharding import PartitionSpec as P

HEAD_DIM = 64
PAIR = 2 * HEAD_DIM
TILE = 16
GRANT = 16 * 1024 * 1024

level_one_bias = math.log(32.0)
level_two_bias = math.log(64.0)
masked_bias = -1e30


def swap_pairs(size):
    return [(i, i ^ 1) for i in range(size)]


def direct_pairs(size):
    return [(i, j) for i in range(size) for j in [i + 2 if i % 2 else i - 2] if 0 <= j < size]


def inverse(pairs):
    return [(j, i) for i, j in pairs]


def shift_pairs(size, shift):
    return [(i, (i + 2 * shift) % size) for i in range(size)]


def both_levels(shift, pair_count):
    return shift == 2 or shift == pair_count - 2


def dot(a, b):
    return jnp.dot(a, b, preferred_element_type=jnp.float32)


def block_diagonal(both):
    top, bottom = (both[:HEAD_DIM], both[HEAD_DIM:])
    zero = jnp.zeros_like(top)
    return jnp.concatenate(
        [jnp.concatenate([top, zero], axis=1), jnp.concatenate([zero, bottom], axis=1)], axis=0
    )


def stacked_heads(both):
    lane = lax.broadcasted_iota(jnp.int32, both.shape, 1)
    first = lane < HEAD_DIM
    zero = jnp.zeros_like(both)
    return jnp.concatenate([jnp.where(first, both, zero), jnp.where(first, zero, both)], axis=0)


def head_rows(both, h):
    return both[h * HEAD_DIM : (h + 1) * HEAD_DIM]


class Unit:
    def __init__(self, query, cotangent, keys, values, keys_t, values_t, bias):
        scaled = query.astype(jnp.float32) * (1.0 / math.sqrt(HEAD_DIM))
        scaled = scaled.astype(jnp.bfloat16)
        self.rows = query.shape[0]
        self.keys, self.values, self.keys_t, self.values_t = (keys, values, keys_t, values_t)
        self.bias = bias
        self.query_wide = block_diagonal(scaled.T)
        self.query_tall = stacked_heads(scaled)
        self.cotangent_t = cotangent.T.astype(jnp.float32)
        self.scores = {}
        self.highest = None
        self.total = 0.0
        self.weights = {}
        self.raw = [0.0, 0.0]
        self.grad_q_t = [0.0, 0.0]
        self.grads = []

    def columns(self, h):
        return slice(h * self.rows, (h + 1) * self.rows)

    def score(self, part):
        score = dot(self.keys[part], self.query_wide)
        plain = max(0, self.keys.shape[0] - self.bias.shape[0] - part.start)
        if plain < score.shape[0]:
            skip = part.start + plain - (self.keys.shape[0] - self.bias.shape[0])
            biased = score[plain:] + self.bias[skip : skip + score.shape[0] - plain]
            score = jnp.concatenate([score[:plain], biased], axis=0) if plain else biased
        highest = jnp.max(score, axis=0, keepdims=True)
        self.highest = highest if self.highest is None else jnp.maximum(self.highest, highest)
        self.scores[part.start] = score

    def weigh(self, part):
        score = self.scores[part.start]
        parts = []
        for start in range(0, score.shape[0], TILE):
            prob = jnp.exp(score[start : start + TILE] - self.highest)
            self.total = self.total + jnp.sum(prob.reshape(-1, 8, prob.shape[1]), axis=0)
            parts.append(prob.astype(jnp.bfloat16))
        weight = jnp.concatenate(parts, axis=0)
        for h in range(2):
            self.raw[h] = self.raw[h] + dot(
                head_rows(self.values_t, h)[:, part], weight[:, self.columns(h)]
            )
        self.weights[part.start] = weight

    def finish(self):
        share = 1.0 / jnp.sum(self.total, axis=0, keepdims=True)
        shares = [share[:, self.columns(h)] for h in range(2)]
        out_t = jnp.concatenate([self.raw[h] * shares[h] for h in range(2)], axis=0)
        out_t = out_t.astype(jnp.bfloat16)
        self.out = out_t.T
        product = self.cotangent_t * out_t.astype(jnp.float32)
        self.delta = jnp.concatenate(
            [
                jnp.sum(head_rows(product, h), axis=0, keepdims=True) * shares[h]
                for h in range(2)
            ],
            axis=1,
        )
        shared_t = jnp.concatenate(
            [head_rows(self.cotangent_t, h) * shares[h] for h in range(2)], axis=0
        )
        shared_t = shared_t.astype(jnp.bfloat16)
        self.cotangent_wide = block_diagonal(shared_t)
        self.cotangent_tall = stacked_heads(shared_t.T)

    def differentiate(self, part):
        weight = self.weights[part.start]
        dots = dot(self.values[part], self.cotangent_wide)
        parts = []
        for start in range(0, dots.shape[0], TILE):
            rows = slice(start, start + TILE)
            grad = weight[rows].astype(jnp.float32) * (dots[rows] - self.delta)
            parts.append(grad.astype(jnp.bfloat16))
        score_grad = jnp.concatenate(parts, axis=0)
        self.grads.append((dot(score_grad, self.query_tall), dot(weight, self.cotangent_tall)))
        for h in range(2):
            self.grad_q_t[h] = self.grad_q_t[h] + dot(
                head_rows(self.keys_t, h)[:, part], score_grad[:, self.columns(h)]
            )

    def grad_q(self):
        grad_q_t = jnp.concatenate(self.grad_q_t, axis=0) * (1.0 / math.sqrt(HEAD_DIM))
        return grad_q_t.astype(jnp.bfloat16).T

    def key_grad(self, n):
        return jnp.concatenate([grads[n] for grads in self.grads], axis=0)


def attention_kernel(shifts, one_rows, two_rows):
    def kernel(
        place, q, k, v, c, pair_k, pair_v, relayed_k, relayed_v, pair_qc, direct, pair_coarse, *rest
    ):
        coarse = rest[:shifts]
        out, grad_q, pair_out, home_grad, pair_grad, direct_grad, relayed_grad = rest[
            shifts : shifts + 7
        ]
        coarse_grads = rest[shifts + 7 :]
        rows = q.shape[0]

        parity, pair = (place[0], place[3])

        def halo(have):
            return jnp.full((rows, 2 * rows), jnp.where(have > 0, 0.0, masked_bias), jnp.float32)

        sizes = [ref.shape[2] for ref in coarse]
        starts = [sum(sizes[:m]) for m in range(shifts + 1)]

        def coarse_bias(query_block):
            pieces = []
            for side in (parity, 1 - parity):
                for shift, size in enumerate(sizes, start=1):
                    row = lax.broadcasted_iota(jnp.int32, (size, 2 * rows), 0)
                    sender = jnp.where(pair >= shift, pair - shift, pair - shift + shifts + 1)
                    apart = jnp.abs(2 * sender + side - query_block)
                    one = jnp.where((apart == 2) | (apart == 3), level_one_bias, masked_bias)
                    two = jnp.where(apart >= 4, level_two_bias, masked_bias)
                    if both_levels(shift, shifts + 1):
                        two = jnp.where(row < one_rows + two_rows, two, masked_bias)
                        pieces.append(jnp.where(row < one_rows, one, two))
                    else:
                        near = jnp.abs(sender - pair) == 1
                        one = jnp.where(near, one, masked_bias)
                        two = jnp.where(near, one, two)
                        one = jnp.where(row < one_rows, one, masked_bias)
                        pieces.append(jnp.where(row < two_rows, two, one))
            return jnp.concatenate(pieces, axis=0).astype(jnp.float32)

        def chunk(pieces):
            return jnp.concatenate(pieces, axis=0), jnp.concatenate([a.T for a in pieces], axis=1)

        def shared(n, home, partner):
            far = jnp.concatenate([ref[0, n].astype(jnp.float32) for ref in coarse], axis=0)
            far = jnp.concatenate([far.astype(jnp.bfloat16), pair_coarse[n]], axis=0)
            return chunk([home[...], partner[...]]), chunk([far])

        both_keys, both_values = (shared(0, k, pair_k), shared(1, v, pair_v))

        def key_rows(outer, near_far):
            near, far = near_far
            pieces = [near, chunk([outer]), far]
            return [jnp.concatenate([a[n] for a in pieces], axis=n) for n in range(2)]

        def unit(query, cotangent, outer_k, outer_v, have, bias):
            keys, keys_t = key_rows(outer_k, both_keys)
            values, values_t = key_rows(outer_v, both_values)
            bias = jnp.concatenate([halo(have), bias], axis=0)
            return Unit(query, cotangent, keys, values, keys_t, values_t, bias)

        one = unit(q[...], c[...], relayed_k[...], relayed_v[...], place[1], coarse_bias(2 * pair + parity))
        two = unit(pair_qc[0], pair_qc[1], direct[0], direct[1], place[2], coarse_bias(2 * pair + 1 - parity))
        count = one.keys.shape[0]
        parts = [slice(0, count)]
        for part in parts:
            one.score(part)
        for part in parts:
            two.score(part)
            one.weigh(part)
        one.finish()
        for part in parts:
            one.differentiate(part)
            two.weigh(part)
        two.finish()
        for part in parts:
            two.differentiate(part)
        out[...], grad_q[...] = (one.out, one.grad_q())
        pair_out[0], pair_out[1] = (two.out, two.grad_q())
        for n in range(2):
            first, second = (one.key_grad(n), two.key_grad(n))
            home_grad[n] = first[:rows] + second[:rows]
            pair_grad[n] = first[rows : 2 * rows] + second[rows : 2 * rows]
            relayed_grad[n] = first[2 * rows : 3 * rows].astype(relayed_grad.dtype)
            direct_grad[n] = second[2 * rows : 3 * rows].astype(direct_grad.dtype)
            far_grad = first[3 * rows :] + second[3 * rows :]
            for m, ref in enumerate(coarse_grads):
                cuts = [
                    slice(side * starts[-1] + starts[m], side * starts[-1] + starts[m + 1])
                    for side in range(2)
                ]
                piece = jnp.concatenate([far_grad[cut] for cut in cuts], axis=0)
                ref[n] = piece.astype(ref.dtype)

    return kernel


def attention(
    place, level_rows, q, k, v, c, pair_k, pair_v, relayed_k, relayed_v, pair_qc, direct, pair_coarse, coarse
):
    rows, width = q.shape
    columns = width // 2
    steps = columns // PAIR
    shifts = len(coarse)

    def mine(j, place):
        return place[0] * steps + j

    def flat(index):
        return pl.BlockSpec((rows, PAIR), index)

    def both(shape_rows):
        return pl.BlockSpec((2, shape_rows, PAIR), lambda j, place: (0, 0, j))

    key_count = 3 * rows + 2 * pair_coarse.shape[1]
    products = 6 * 2 * 2 * rows * key_count * HEAD_DIM * 2 * steps
    bf16, f32 = (jnp.bfloat16, jnp.float32)
    return pl.pallas_call(
        attention_kernel(shifts, *level_rows),
        grid_spec=pltpu.PrefetchScalarGridSpec(
            num_scalar_prefetch=1,
            grid=(steps,),
            in_specs=[flat(lambda j, place: (0, mine(j, place)))] * 4
            + [flat(lambda j, place: (0, j))] * 4
            + [both(rows)] * 2
            + [both(pair_coarse.shape[1])]
            + [
                pl.BlockSpec((1, 2, piece.shape[2], PAIR), lambda j, place: (place[0], 0, 0, j))
                for piece in coarse
            ],
            out_specs=[flat(lambda j, place: (0, j))] * 2
            + [both(rows)] * 5
            + [both(2 * piece.shape[2]) for piece in coarse],
        ),
        out_shape=[jax.ShapeDtypeStruct((rows, columns), bf16)] * 2
        + [
            jax.ShapeDtypeStruct((2, rows, columns), bf16),
            jax.ShapeDtypeStruct((2, rows, columns), f32),
            jax.ShapeDtypeStruct((2, rows, columns), f32),
            jax.ShapeDtypeStruct((2, rows, columns), bf16),
            jax.ShapeDtypeStruct((2, rows, columns), bf16),
        ]
        + [jax.ShapeDtypeStruct((2, 2 * piece.shape[2], columns), bf16) for piece in coarse],
        compiler_params=pltpu.CompilerParams(vmem_limit_bytes=GRANT),
        cost_estimate=pl.CostEstimate(
            flops=4 * products, bytes_accessed=40 * rows * columns, transcendentals=0
        ),
        name="attention",
    )(
        place, q, k, v, c, pair_k, pair_v, relayed_k, relayed_v, pair_qc, direct, pair_coarse, *coarse
    )


def restrict_kernel(place, restrict, k, v, spread, *outs):
    half = outs[0].shape[3]
    short = restrict.shape[0] // 2
    pair, shifts = (place[3], len(outs))

    def chosen(rows, shift):
        if both_levels(shift, shifts + 1):
            return rows
        apart = jnp.where(pair + shift <= shifts, shift, shifts + 1 - shift)
        return jnp.where(apart == 1, rows[:short], rows[short:])

    for n, ref in enumerate((k, v)):
        for side in range(2):
            rows = dot(restrict[...], ref[:, side * half : (side + 1) * half])
            for shift, out in enumerate(outs, start=1):
                out[side, n] = chosen(rows, shift).astype(out.dtype)
    whole = restrict[...].astype(jnp.float32)
    spread[...] = jnp.concatenate([chosen(whole, s) for s in range(1, shifts + 1)], axis=0)


def restricted(place, restrict, keys, values, pair_count):
    vmem = pl.BlockSpec(memory_space=pltpu.VMEM)
    rows = restrict.shape[0]
    sizes = [rows if both_levels(s, pair_count) else rows // 2 for s in range(1, pair_count)]
    return pl.pallas_call(
        restrict_kernel,
        in_specs=[pl.BlockSpec(memory_space=pltpu.SMEM)] + [vmem] * 3,
        out_specs=[vmem] * pair_count,
        out_shape=[jax.ShapeDtypeStruct((sum(sizes), restrict.shape[1]), jnp.float32)]
        + [jax.ShapeDtypeStruct((2, 2, size, keys.shape[1] // 2), keys.dtype) for size in sizes],
        compiler_params=pltpu.CompilerParams(vmem_limit_bytes=GRANT),
        name="restrict",
    )(place, restrict, keys, values)


def lengthened(restrict, coarse):
    return jnp.einsum(
        "fb,nfc->nbc", restrict, coarse, precision=lax.Precision.HIGHEST
    )


def per_device(queries, keys, values, cotangent, restrict_one, restrict_two):
    rows, width = queries.shape
    size = lax.axis_size("seq")
    pair_count = size // 2
    position = lax.axis_index("seq")
    parity = lax.rem(position, 2)
    pair = lax.div(position, 2)
    one_rows, two_rows = (restrict_one.shape[0], restrict_two.shape[0])
    short = max(one_rows, two_rows)
    block_rows = 2 * short
    restrict = jnp.concatenate(
        [
            jnp.pad(restrict_one, ((0, short - one_rows), (0, 0))),
            jnp.pad(restrict_two, ((0, short - two_rows), (0, 0))),
        ],
        axis=0,
    )

    has_before, has_after = (pair > 0, pair < pair_count - 1)
    place = jnp.stack(
        [
            parity,
            jnp.where(parity == 0, has_before, has_after).astype(jnp.int32),
            jnp.where(parity == 0, has_after, has_before).astype(jnp.int32),
            pair,
        ]
    ).astype(jnp.int32)

    direct_to = direct_pairs(size)
    relayed_to = inverse(direct_to)
    swap = swap_pairs(size)

    def send(value, pairs):
        return lax.ppermute(value, "seq", pairs)

    half = width // 2
    shifts = range(1, pair_count)

    def columns(side, *arrays):
        return [lax.dynamic_slice_in_dim(a, side * half, half, axis=a.ndim - 1) for a in arrays]

    def after(value, *others):
        return lax.optimization_barrier((value, *others))[0]

    pair_k, pair_v = (send(a, swap) for a in columns(1 - parity, keys, values))
    spread, *own_coarse = restricted(place, restrict, keys, values, pair_count)
    own_coarse = after(own_coarse, pair_k)
    coarse = [send(a, shift_pairs(size, s)) for s, a in zip(shifts, own_coarse)]
    relayed_k = send(pair_k, relayed_to)
    home_kv = jnp.stack(columns(parity, keys, values))
    direct = send(after(home_kv, coarse[0]), direct_to)
    sent_qc = jnp.stack(columns(1 - parity, queries, cotangent))
    pair_qc = send(after(sent_qc, pair_v), swap)
    relayed_v = send(after(pair_v, relayed_k), relayed_to)
    sent_coarse = jnp.concatenate(
        [
            lax.dynamic_slice_in_dim(a, 1 - parity, 1).reshape(a.shape[1:])
            for a in after(coarse, pair_v)
        ],
        axis=1,
    )
    pair_coarse = send(sent_coarse, swap)
    direct = after(direct, pair_qc)
    relayed_v = after(relayed_v, direct)

    (
        out, grad_q, pair_out, home_grad, pair_grad, direct_grad, relayed_grad, *coarse_grads,
    ) = attention(
        place, (one_rows, two_rows), queries, keys, values, cotangent,
        pair_k, pair_v, relayed_k, relayed_v, pair_qc, direct, pair_coarse, coarse,
    )

    def whole(own, other):
        axis = own.ndim - 1
        return jnp.where(
            parity == 0,
            jnp.concatenate([own, other], axis=axis),
            jnp.concatenate([other, own], axis=axis),
        )

    relayed_back = send(relayed_grad, direct_to)
    out_back = send(pair_out, swap)
    pair_total = (pair_grad + relayed_back.astype(jnp.float32)).astype(jnp.bfloat16)
    grad_back = send(pair_total, swap)
    coarse_grads[-1] = after(coarse_grads[-1], pair_total)
    coarse_back = [send(a, shift_pairs(size, -s)) for s, a in zip(shifts, coarse_grads)]
    direct_back = send(direct_grad, relayed_to)
    far = [
        piece.astype(jnp.float32).reshape(2, 2, -1, half)
        for piece in after(coarse_back, pair_total)
    ]
    far = [jnp.concatenate([piece[:, side] for piece in far], axis=1) for side in range(2)]
    sent_far = far[1].astype(jnp.bfloat16)
    other_far = send(sent_far, swap).astype(jnp.float32)
    other_longer = lax.optimization_barrier(lengthened(spread, other_far))
    home_total = home_grad + direct_back.astype(jnp.float32)
    home_total = (home_total + lengthened(spread, far[0])).astype(jnp.bfloat16)
    pair_back = (grad_back.astype(jnp.float32) + other_longer).astype(jnp.bfloat16)
    return (
        whole(out, out_back[0]),
        whole(grad_q, out_back[1]),
        whole(home_total[0], pair_back[0]),
        whole(home_total[1], pair_back[1]),
    )


def solution(mesh):
    split = P(("prompt", "seq"), None)
    return jax.shard_map(
        per_device,
        mesh=mesh,
        in_specs=(split, split, split, split, P(), P()),
        out_specs=(split, split, split, split),
        check_vma=False,
    )
```
